32 devices in a mesh: dop: 8 (over z, x), rng: 4 (over y, core).
Axes of the slice: x: 2, y: 2, z: 4, core: 2. Of those that a mesh axis runs over, the one named last changes fastest.
Arguments:
- raw_samples: bfloat16 [256, 96, 2, 4096], P('dop', 'rng'), may hold values from -16 to 16
- filter_taps: float32 [8, 512], replicated, may hold values from -2 to 2
- range_code: float32 [2, 7], replicated, may hold values from -1.6 to 1.6
- train_mask: int32 [16, 96], P('dop', 'rng'), may hold values 0 or 1
- steer_index: int32 [16, 4], P('dop'), may hold values from 0 to 255
Outputs:
- beam_out: float32 [2, 16, 4, 96], P(None, 'dop', None, 'rng')
The draws below stay inside these ranges and needn't reach their ends.
All inputs are finite; a program needn't handle non-finite values. No bound on the sum of `train_mask` on one device may be relied on, other than what follows from the above.
Results may differ from the reference program's by a relative error of at most 0.012.
The reference program's roundings to bfloat16 on the way (of `filtered`, `dft_table`, `spectra` and `compressed`) count: a program that leaves them out, or rounds other values in their place, can miss the bound.
Values may be sent and summed in bfloat16 or wider, within the bound.
A program may use at most 128 MiB of HBM per device.

```python
import math
import jax
import jax.numpy as jnp
from jax import lax

ELEMENTS = 256
CHANNELS = 512
TAPS = 8
CODE_REACH = 3
BEAMS = 4
PULSES = 4096
BINS = 16
GATES = 96


def draw_raw_samples(key, part):
    source_count = max(ELEMENTS // 4, 4)
    strongest = 4.0
    decades = 3.5
    direction_key = jax.random.fold_in(key, 11)
    power_key = jax.random.fold_in(key, 12)
    signal_key = jax.random.fold_in(key, 13)
    noise_key = jax.random.fold_in(key, 14)
    sine_values = jax.random.uniform(direction_key, (source_count,), jnp.float32, -0.95, 0.95)
    spacing = (jnp.arange(source_count, dtype=jnp.float32) + jax.random.uniform(power_key, (source_count,), jnp.float32)) / source_count
    amplitude = jnp.sqrt(0.5 * strongest * 10.0 ** (-decades * spacing))
    positions = jnp.arange(ELEMENTS, dtype=jnp.float32)
    phases = math.pi * positions[:, None] * sine_values[None, :]
    cosine = jnp.cos(phases) * amplitude[None, :]
    sine_part = jnp.sin(phases) * amplitude[None, :]
    real_row = jnp.stack([cosine, -sine_part], axis=2)
    imag_row = jnp.stack([sine_part, cosine], axis=2)
    mixing = jnp.stack([real_row, imag_row], axis=1).reshape(2 * ELEMENTS, 2 * source_count)

    def one_gate(gate_number):
        source_key = jax.random.fold_in(signal_key, gate_number)
        floor_key = jax.random.fold_in(noise_key, gate_number)
        sources = jax.random.normal(source_key, (2 * source_count, PULSES), jnp.float32)
        noise_part = jax.random.normal(floor_key, (2 * ELEMENTS, PULSES), jnp.float32) * math.sqrt(0.5)
        combined = jnp.dot(mixing, sources, precision=lax.Precision.HIGHEST) + noise_part
        return jnp.clip(combined, -16.0, 16.0).reshape(ELEMENTS, 2, PULSES).astype(jnp.bfloat16)
    per_gate = lax.map(one_gate, jnp.arange(GATES, dtype=jnp.int32))
    return jnp.transpose(per_gate, (1, 0, 2, 3))


def set_ends(array, key, low, high):
    spot = [jax.random.randint(jax.random.fold_in(key, axis), (), 0, length) for axis, length in enumerate(array.shape)]
    longest = array.shape.index(max(array.shape))
    neighbour = spot[:longest] + [(spot[longest] + 1) % array.shape[longest]] + spot[longest + 1:]
    return array.at[tuple(spot)].set(low).at[tuple(neighbour)].set(high)


def noise(stream_key, dims, width, limit, held_as=jnp.bfloat16):
    return jnp.clip(width * jax.random.normal(stream_key, dims, jnp.float32), -limit, limit).astype(held_as)


def setup_inputs(seed: int = 0) -> dict:
    key_of = jax.random.split(jax.random.key(seed), 6)
    raw_samples = draw_raw_samples(jax.random.fold_in(key_of[5], 71), 0)
    filter_taps = noise(key_of[1], (TAPS, CHANNELS), TAPS ** -0.5, 2.0, jnp.float32)
    range_code = noise(key_of[2], (2, 2 * CODE_REACH + 1), 0.27, 1.6, jnp.float32)
    train_mask = set_ends((jax.random.randint(key_of[3], (BINS, GATES), 0, 4) < 3).astype(jnp.int32), jax.random.fold_in(key_of[3], 1), 0, 1)
    steer_index = set_ends(jax.random.randint(key_of[4], (BINS, BEAMS), 0, ELEMENTS), jax.random.fold_in(key_of[4], 1), 0, ELEMENTS - 1).astype(jnp.int32)
    return {"raw_samples": raw_samples, "filter_taps": filter_taps, "range_code": range_code, "train_mask": train_mask, "steer_index": steer_index}


loading_level = 0.25

def dft_table(bin_total):
    mode_index = jnp.arange(CHANNELS, dtype=jnp.int32)
    bin_index = jnp.arange(bin_total, dtype=jnp.int32)
    turn_count = jnp.mod(mode_index[:, None] * bin_index[None, :], CHANNELS).astype(jnp.float32)
    phases = turn_count * (2.0 * math.pi / CHANNELS)
    cosine = jnp.cos(phases) / math.sqrt(CHANNELS)
    sine_part = jnp.sin(phases) / math.sqrt(CHANNELS)
    top_half = jnp.concatenate([cosine, -sine_part], axis=1)
    low_half = jnp.concatenate([sine_part, cosine], axis=1)
    return jnp.concatenate([top_half, low_half], axis=0).astype(jnp.bfloat16)

def channelize(samples, filter_taps, table):
    gate_count = samples.shape[0]
    folded = samples.astype(jnp.float32).reshape(gate_count, 2, TAPS, CHANNELS)
    filtered = lax.optimization_barrier(jnp.sum(folded * filter_taps, axis=2)).astype(jnp.bfloat16)
    flattened = filtered.reshape(gate_count, 2 * CHANNELS)
    spectra = jnp.dot(flattened.astype(jnp.float32), table.astype(jnp.float32), preferred_element_type=jnp.float32)
    return spectra.astype(jnp.bfloat16).reshape(gate_count, 2, BINS)

def compress(padded, range_code):
    gate_count = padded.shape[1] - 2 * CODE_REACH
    shape_out = (padded.shape[0], gate_count, padded.shape[3])
    real_sum = jnp.zeros(shape_out, jnp.float32)
    imag_sum = jnp.zeros(shape_out, jnp.float32)
    for offset in range(2 * CODE_REACH + 1):
        window = lax.slice_in_dim(padded, offset, offset + gate_count, axis=1).astype(jnp.float32)
        real_sum = real_sum + range_code[0, offset] * window[:, :, 0] - range_code[1, offset] * window[:, :, 1]
        imag_sum = imag_sum + range_code[0, offset] * window[:, :, 1] + range_code[1, offset] * window[:, :, 0]
    return jnp.stack([real_sum, imag_sum], axis=2).astype(jnp.bfloat16)

def local_gram(masked):
    real_rows = masked[:, :, 0]
    imag_rows = masked[:, :, 1]
    top_rows = jnp.concatenate([real_rows, imag_rows], axis=2)
    low_rows = jnp.concatenate([-imag_rows, real_rows], axis=2)
    stacked = jnp.concatenate([top_rows, low_rows], axis=1).astype(jnp.float32)
    return jnp.einsum('bri,brj->bij', stacked, stacked, precision=lax.Precision.HIGHEST)

def steering_table(steer_rows):
    element = jnp.arange(ELEMENTS, dtype=jnp.int32)
    turn_count = jnp.mod(element[None, :, None] * (2 * steer_rows[:, None, :] - ELEMENTS), 2 * ELEMENTS).astype(jnp.float32)
    phases = turn_count * (math.pi / ELEMENTS)
    return jnp.concatenate([jnp.cos(phases), jnp.sin(phases)], axis=1)

def solve_all(factor, steering):
    return jax.vmap(lambda lower_part, target: jax.scipy.linalg.cho_solve((lower_part, True), target))(factor, steering)

def beam_output(compressed, weights, steering):
    response = lax.optimization_barrier(jnp.sum(steering * weights, axis=1))
    signal = compressed.astype(jnp.float32)
    weight_real = weights[:, :ELEMENTS]
    weight_imag = weights[:, ELEMENTS:]
    highest = lax.Precision.HIGHEST
    out_real = jnp.einsum('bik,bgi->bkg', weight_real, signal[:, :, 0], precision=highest) + jnp.einsum('bik,bgi->bkg', weight_imag, signal[:, :, 1], precision=highest)
    out_imag = jnp.einsum('bik,bgi->bkg', weight_real, signal[:, :, 1], precision=highest) - jnp.einsum('bik,bgi->bkg', weight_imag, signal[:, :, 0], precision=highest)
    return jnp.stack([out_real, out_imag], axis=0) / jnp.sqrt(response)[None, :, :, None]

def adapt_one(inputs):
    compressed, mask_row, steer_row = inputs
    compressed = compressed[None]
    masked = compressed * mask_row.astype(jnp.bfloat16)[None, :, None, None]
    identity = jnp.eye(2 * ELEMENTS, dtype=jnp.float32)
    gram = local_gram(masked) / GATES + loading_level * identity
    factor = jnp.linalg.cholesky(gram)
    steering = steering_table(steer_row[None])
    weights = solve_all(factor, steering)
    return beam_output(compressed, weights, steering)[:, 0]

def reference(raw_samples, filter_taps, range_code, train_mask, steer_index):
    table = dft_table(BINS)
    per_element = lax.map(lambda samples: channelize(samples, filter_taps, table), raw_samples)
    spectra = jnp.transpose(per_element, (3, 1, 2, 0))
    padded = jnp.pad(spectra, ((0, 0), (CODE_REACH, CODE_REACH), (0, 0), (0, 0)))
    compressed = compress(padded, range_code)
    outputs = lax.map(adapt_one, (compressed, train_mask, steer_index))
    return jnp.transpose(outputs, (1, 0, 2, 3))
```

```python
import math

import jax
import jax.numpy as jnp
from jax import lax
from jax.experimental import pallas as pl
from jax.experimental.pallas import tpu as pltpu
from jax.sharding import PartitionSpec as P

ELEMENTS = 256
CHANNELS = 512
TAPS = 8
CODE_REACH = 3


loading_level = 0.25


def padded_2(x, sides, width):
    for axis, dim in sides:
        count, length = (lax.axis_size(axis), x.shape[dim])
        up = [(i, (i + 1) % count) for i in range(count - 1)]
        down = [(j, i) for i, j in up]
        last = lax.slice_in_dim(x, length - width, length, axis=dim)
        leading = lax.slice_in_dim(x, 0, width, axis=dim)
        before = lax.ppermute(last, axis, up)
        after = lax.ppermute(leading, axis, down)
        x = jnp.concatenate([before, x, after], axis=dim)
    return x


def dft_table(bin_total):
    mode_index = jnp.arange(CHANNELS, dtype=jnp.int32)
    bin_index = jnp.arange(bin_total, dtype=jnp.int32)
    turn_count = jnp.mod(mode_index[:, None] * bin_index[None, :], CHANNELS).astype(jnp.float32)
    phases = turn_count * (2.0 * math.pi / CHANNELS)
    cosine = jnp.cos(phases) / math.sqrt(CHANNELS)
    sine_part = jnp.sin(phases) / math.sqrt(CHANNELS)
    top_half = jnp.concatenate([cosine, -sine_part], axis=1)
    low_half = jnp.concatenate([sine_part, cosine], axis=1)
    return jnp.concatenate([top_half, low_half], axis=0).astype(jnp.bfloat16)


def compress(padded, range_code):
    gate_count = padded.shape[1] - 2 * CODE_REACH
    shape_out = (padded.shape[0], gate_count, padded.shape[3])
    real_sum = jnp.zeros(shape_out, jnp.float32)
    imag_sum = jnp.zeros(shape_out, jnp.float32)
    for offset in range(2 * CODE_REACH + 1):
        window = lax.slice_in_dim(padded, offset, offset + gate_count, axis=1).astype(jnp.float32)
        real_sum = (
            real_sum
            + range_code[0, offset] * window[:, :, 0]
            - range_code[1, offset] * window[:, :, 1]
        )
        imag_sum = (
            imag_sum
            + range_code[0, offset] * window[:, :, 1]
            + range_code[1, offset] * window[:, :, 0]
        )
    return jnp.stack([real_sum, imag_sum], axis=2).astype(jnp.bfloat16)


def local_gram(masked):
    real_rows = masked[:, :, 0]
    imag_rows = masked[:, :, 1]
    top_rows = jnp.concatenate([real_rows, imag_rows], axis=2)
    low_rows = jnp.concatenate([-imag_rows, real_rows], axis=2)
    stacked = jnp.concatenate([top_rows, low_rows], axis=1)
    return jnp.einsum("bri,brj->bij", stacked, stacked, preferred_element_type=jnp.float32)


def steering_table(steer_rows):
    element = jnp.arange(ELEMENTS, dtype=jnp.int32)
    turn_count = jnp.mod(
        element[None, :, None] * (2 * steer_rows[:, None, :] - ELEMENTS), 2 * ELEMENTS
    ).astype(jnp.float32)
    phases = turn_count * (math.pi / ELEMENTS)
    return jnp.concatenate([jnp.cos(phases), jnp.sin(phases)], axis=1)


def solve_all(factor, steering):
    return jax.vmap(
        lambda lower_part, target: jax.scipy.linalg.cho_solve((lower_part, True), target)
    )(factor, steering)


def beam_output(compressed, weights, steering):
    response = jnp.sum(steering * weights, axis=1)
    signal = compressed.astype(jnp.float32)
    weight_real = weights[:, :ELEMENTS]
    weight_imag = weights[:, ELEMENTS:]
    highest = lax.Precision.HIGHEST
    out_real = jnp.einsum(
        "bik,bgi->bkg", weight_real, signal[:, :, 0], precision=highest
    ) + jnp.einsum("bik,bgi->bkg", weight_imag, signal[:, :, 1], precision=highest)
    out_imag = jnp.einsum(
        "bik,bgi->bkg", weight_real, signal[:, :, 1], precision=highest
    ) - jnp.einsum("bik,bgi->bkg", weight_imag, signal[:, :, 0], precision=highest)
    return jnp.stack([out_real, out_imag], axis=0) / jnp.sqrt(response)[None, :, :, None]


def plain_shards(raw_samples, filter_taps, range_code, train_mask, steer_index):
    elem_dev = raw_samples.shape[0]
    gate_dev = raw_samples.shape[1]
    bin_dev = train_mask.shape[0]
    bin_total = bin_dev * lax.axis_size("dop")
    gates_total = gate_dev * lax.axis_size("rng")
    table = dft_table(bin_total)
    folded = raw_samples.astype(jnp.float32).reshape(elem_dev, gate_dev, 2, TAPS, CHANNELS)
    filtered = jnp.sum(folded * filter_taps, axis=3).astype(jnp.bfloat16)
    spectra = jnp.dot(
        filtered.reshape(elem_dev * gate_dev, 2 * CHANNELS),
        table,
        preferred_element_type=jnp.float32,
    )
    spectra = jnp.transpose(
        spectra.astype(jnp.bfloat16).reshape(elem_dev, gate_dev, 2, bin_total), (3, 1, 2, 0)
    )
    turned = lax.all_to_all(spectra, "dop", split_axis=0, concat_axis=3, tiled=True)
    padded = padded_2(turned, (("rng", 1),), CODE_REACH)
    compressed = compress(padded, range_code)
    masked = compressed * train_mask.astype(jnp.bfloat16)[:, :, None, None]
    dof_count = 2 * ELEMENTS
    identity = jnp.eye(dof_count, dtype=jnp.float32)
    steering = steering_table(steer_index)
    range_count = lax.axis_size("rng")
    owned_count = (bin_dev + range_count - 1) // range_count
    padded_bins = owned_count * range_count
    filled = jnp.pad(masked, ((0, padded_bins - bin_dev), (0, 0), (0, 0), (0, 0)))
    owned_rows = lax.all_to_all(filled, "rng", split_axis=0, concat_axis=1, tiled=True)
    owned_gram = local_gram(owned_rows) / gates_total + loading_level * identity
    owned_factor = jnp.linalg.cholesky(owned_gram)
    steer_filled = jnp.pad(steer_index, ((0, padded_bins - bin_dev), (0, 0)))
    first_bin = lax.axis_index("rng") * owned_count
    owned_steer = lax.dynamic_slice_in_dim(steer_filled, first_bin, owned_count, 0)
    owned_weights = solve_all(owned_factor, steering_table(owned_steer))
    weights = lax.all_gather(owned_weights, "rng", axis=0, tiled=True)[:bin_dev]
    return beam_output(compressed, weights, steering)


LANES = 128
MESH = pl.DeviceIdType.MESH
NT = (((1,), (1,)), ((), ()))


def pair_swapped(x, lane, slot):
    imag = jnp.mod(lane // slot, 2) == 1
    return jnp.where(imag, pltpu.roll(x, slot, 1), -pltpu.roll(x, LANES - slot, 1))


def channelize_kernel(raw_ref, taps_ref, table_ref, out_ref, filt_ref, spec_ref):
    elems, gates = raw_ref.shape[0], raw_ref.shape[1]
    dops, rows = out_ref.shape[0], out_ref.shape[1]
    step, steps = pl.program_id(0), pl.num_programs(0)
    for gate in range(gates):

        def one(e, carry, gate=gate):
            x = raw_ref[e, gate].astype(jnp.float32).reshape(TAPS, 8, LANES)
            at = pl.multiple_of((gate * elems + e) * 8, 8)
            filt_ref[pl.ds(at, 8), :] = jnp.sum(x * taps_ref[...], axis=0)
            return carry

        lax.fori_loop(0, elems, one, 0, unroll=8)
    parts = [
        filt_ref[pl.ds(i, gates * elems, stride=8), :].astype(jnp.bfloat16) for i in range(8)
    ]
    chunk = lax.dot_general(
        table_ref[...], jnp.concatenate(parts, axis=1), NT, preferred_element_type=jnp.float32
    )
    lane = lax.broadcasted_iota(jnp.int32, (dops, LANES), 1)
    for q in range(gates):
        row = jnp.zeros((dops, LANES), jnp.float32)
        for c in range(LANES // elems):
            piece = chunk[c * dops : (c + 1) * dops]
            shift = ((c - q) * elems) % LANES
            if shift:
                piece = pltpu.roll(piece, shift, 1)
            row = jnp.where(lane // elems == c, piece, row)
        at = pl.multiple_of((step * gates + q) * dops, 8)
        spec_ref[pl.ds(at, dops), :] = row

    @pl.when(step == steps - 1)
    def _():
        full = steps * gates
        if rows > full:
            spec_ref[pl.ds(full * dops, (rows - full) * dops), :] = jnp.zeros(
                ((rows - full) * dops, LANES), jnp.float32
            )
        for d in range(dops):
            out_ref[d] = spec_ref[pl.ds(d, rows, stride=dops), :].astype(jnp.bfloat16)


def channelize(raw, filter_taps, bin_total, dops, rows):
    elems, gates = raw.shape[0], raw.shape[1]
    bin_dev = bin_total // dops
    quarters = CHANNELS // LANES
    view = raw.reshape(elems, gates, 2, TAPS * quarters, LANES)
    view = jnp.transpose(view, (0, 1, 3, 2, 4)).reshape(elems, gates, 2 * TAPS * quarters, LANES)
    taps = filter_taps.reshape(TAPS, quarters, 1, LANES)
    taps = jnp.broadcast_to(taps, (TAPS, quarters, 2, LANES)).reshape(TAPS, 2 * quarters, LANES)
    table = dft_table(bin_total).reshape(2, quarters, LANES, 2, dops, bin_dev)
    table = jnp.transpose(table, (5, 3, 4, 1, 0, 2)).reshape(2 * bin_total, 2 * CHANNELS)
    block = LANES // elems
    return pl.pallas_call(
        channelize_kernel,
        grid=(gates // block,),
        in_specs=[
            pl.BlockSpec((elems, block, 2 * TAPS * quarters, LANES), lambda i: (0, i, 0, 0)),
            pl.BlockSpec(taps.shape, lambda i: (0, 0, 0)),
            pl.BlockSpec(table.shape, lambda i: (0, 0)),
        ],
        out_specs=pl.BlockSpec((dops, rows, LANES), lambda i: (0, 0, 0)),
        out_shape=jax.ShapeDtypeStruct((dops, rows, LANES), jnp.bfloat16),
        scratch_shapes=[
            pltpu.VMEM((elems * block * 8, LANES), jnp.float32),
            pltpu.VMEM((rows * dops, LANES), jnp.float32),
        ],
        compiler_params=pltpu.CompilerParams(vmem_limit_bytes=56 * 1024 * 1024),
    )(view, taps, table)


def exchange_kernel(dops, rngs, spec_ref, mask_ref, out_ref, send1, recv1, send2, recv2):
    d, r = lax.axis_index("dop"), lax.axis_index("rng")
    barrier = pltpu.get_barrier_semaphore()
    for i in range(1, dops):
        pl.semaphore_signal(
            barrier, inc=1, device_id=(lax.rem(d + i, dops), r), device_id_type=MESH
        )
    for j in range(1, rngs):
        pl.semaphore_signal(
            barrier, inc=1, device_id=(d, lax.rem(r + j, rngs)), device_id_type=MESH
        )
    pl.semaphore_wait(barrier, dops + rngs - 2)
    out_ref[d, r] = spec_ref[d]
    out_ref[dops, r] = mask_ref[...]
    turns = []
    for i in range(1, dops):
        to = lax.rem(d + i, dops)
        turns.append(
            pltpu.make_async_remote_copy(
                src_ref=spec_ref.at[to],
                dst_ref=out_ref.at[d, r],
                send_sem=send1.at[i],
                recv_sem=recv1.at[i],
                device_id=(to, r),
                device_id_type=MESH,
            )
        )
        turns[-1].start()
    passed = []

    def forward(block, i):
        for j in range(1, rngs):
            copy = pltpu.make_async_remote_copy(
                src_ref=out_ref.at[block, r],
                dst_ref=out_ref.at[block, r],
                send_sem=send2.at[i, j],
                recv_sem=recv2.at[i, j],
                device_id=(d, lax.rem(r + j, rngs)),
                device_id_type=MESH,
            )
            copy.start()
            passed.append(copy)

    forward(d, 0)
    forward(dops, dops)
    for i in range(1, dops):
        turns[i - 1].wait_recv()
        forward(lax.rem(d + dops - i, dops), i)
    for copy in passed:
        copy.wait_recv()
    for copy in turns + passed:
        copy.wait_send()


def exchange(spectra, mask_rows, dops, rngs):
    shape = (dops + 1, rngs) + mask_rows.shape
    return pl.pallas_call(
        lambda *refs: exchange_kernel(dops, rngs, *refs),
        in_specs=[pl.BlockSpec(memory_space=pltpu.VMEM)] * 2,
        out_specs=pl.BlockSpec(memory_space=pltpu.VMEM),
        out_shape=jax.ShapeDtypeStruct(shape, jnp.bfloat16),
        scratch_shapes=[
            pltpu.SemaphoreType.DMA((dops,)),
            pltpu.SemaphoreType.DMA((dops,)),
            pltpu.SemaphoreType.DMA((dops + 1, rngs)),
            pltpu.SemaphoreType.DMA((dops + 1, rngs)),
        ],
        compiler_params=pltpu.CompilerParams(collective_id=0, has_side_effects=True),
    )(spectra, mask_rows)


def eliminate(problems):
    states = []
    for a_re, a_im, b_re, b_im in problems:
        size = a_re.shape[0]
        tiles = [
            [a_re[i : i + 8], a_im[i : i + 8]] for i in range(0, size, 8)
        ] + [[b_re, b_im]]
        states.append(tiles)
    lanes = {
        rows: lax.broadcasted_iota(jnp.int32, (rows, size), 1) for rows in (1, 8, b_re.shape[0])
    }
    for p in range(size):
        first, s = divmod(p, 8)
        for tiles in states:
            row_re, row_im = (part[s : s + 1] for part in tiles[first])
            inverse = 1.0 / row_re[:, p : p + 1]
            here = lanes[1] == p
            row_re = jnp.where(here, -inverse, row_re * inverse)
            row_im = jnp.where(here, 0.0, row_im * inverse)
            begin = first + 1 if s == 7 else first
            for tile in tiles[begin:]:
                t_re, t_im = tile
                c_re, c_im = t_re[:, p : p + 1], t_im[:, p : p + 1]
                at = lanes[t_re.shape[0]] == p
                tile[0] = jnp.where(at, 0.0, t_re) - (c_re * row_re - c_im * row_im)
                tile[1] = jnp.where(at, 0.0, t_im) - (c_re * row_im + c_im * row_re)
    return [tiles[-1] for tiles in states]


def adapt_kernel(gate_dev, bin_dev, code_ref, steer_ref, rows_ref, out_ref, self_ref, turned_ref):
    dops, rngs = rows_ref.shape[0] - 1, rows_ref.shape[1]
    gates = gate_dev * rngs
    slot = LANES // (2 * bin_dev)
    lane_dev = lax.broadcasted_iota(jnp.int32, (gate_dev, LANES), 1)
    lane = lax.broadcasted_iota(jnp.int32, (gates, LANES), 1)
    mask = jnp.concatenate(
        [rows_ref[dops, r].astype(jnp.float32)[:gate_dev] for r in range(rngs)], axis=0
    )
    signal, turned, train, train_turned = [], [], [], []
    edge = jnp.zeros((8, LANES), jnp.float32)
    for d in range(dops):
        for ref in (self_ref, turned_ref):
            ref[d, 0:8] = edge
            ref[d, 8 + gates : 16 + gates] = edge
        for r in range(rngs):
            y = rows_ref[d, r].astype(jnp.float32)[:gate_dev]
            at = 8 + r * gate_dev
            self_ref[d, at : at + gate_dev] = y
            turned_ref[d, at : at + gate_dev] = pair_swapped(y, lane_dev, slot)
        total = jnp.zeros((gates, LANES), jnp.float32)
        for t in range(2 * CODE_REACH + 1):
            at = 8 - CODE_REACH + t
            total = (
                total
                + code_ref[0, t] * self_ref[d, at : at + gates]
                + code_ref[1, t] * turned_ref[d, at : at + gates]
            )
        v = total.astype(jnp.bfloat16).astype(jnp.float32)
        q = pair_swapped(v, lane, slot)
        signal.append(v.astype(jnp.bfloat16))
        turned.append(q.astype(jnp.bfloat16))
        train.append((v * mask).astype(jnp.bfloat16))
        train_turned.append((q * mask).astype(jnp.bfloat16))

    def dot(a, b):
        return lax.dot_general(a, b, NT, preferred_element_type=jnp.float32)

    def of_bins(parts):
        rows = []
        for k in range(bin_dev):
            own = lane // (2 * slot) == k
            rows.append(
                jnp.concatenate(
                    [jnp.where(own, x.astype(jnp.float32), 0.0).astype(jnp.bfloat16) for x in parts],
                    axis=1,
                )
            )
        return jnp.concatenate(rows, axis=0)

    signal_bins, train_bins = of_bins(signal), of_bins(train)
    signal, turned, train, train_turned = (
        jnp.concatenate(x, axis=1) for x in (signal, turned, train, train_turned)
    )
    all_re, all_im = dot(signal_bins, signal), dot(signal_bins, turned)
    gram_re, gram_im = dot(train_bins, train), dot(train_bins, train_turned)
    steer = steer_ref[...]
    high = steer.astype(jnp.bfloat16)
    rest = steer - high.astype(jnp.float32)
    middle = rest.astype(jnp.bfloat16)
    low = (rest - middle.astype(jnp.float32)).astype(jnp.bfloat16)
    looks = dot(high, signal) + (dot(middle, signal) + dot(low, signal))
    sights = dot(high, train) + (dot(middle, train) + dot(low, train))
    norms = jnp.sum(steer * steer, axis=1, keepdims=True)
    beams = steer.shape[0] // (2 * bin_dev)
    diagonal = (
        lax.broadcasted_iota(jnp.int32, (gates, gates), 0)
        == lax.broadcasted_iota(jnp.int32, (gates, gates), 1)
    )
    loading = jnp.where(diagonal, loading_level * gates, 0.0)
    problems = []
    for k in range(bin_dev):
        at, b = k * gates, 2 * k * beams
        problems.append(
            (
                gram_re[at : at + gates] + loading,
                -gram_im[at : at + gates],
                sights[b : b + beams],
                sights[b + beams : b + 2 * beams],
            )
        )
    solved = eliminate(problems)
    place = lax.axis_index("rng")
    highest = lax.Precision.HIGHEST
    for k in range(bin_dev):
        y_re, y_im = solved[k]
        b_re, b_im = problems[k][2:]
        at, b = k * gates, 2 * k * beams
        k_re, k_im = all_re[at : at + gates], all_im[at : at + gates]
        both = jnp.concatenate([y_re, y_im], axis=0)
        by_re = jnp.dot(both, k_re, precision=highest, preferred_element_type=jnp.float32)
        by_im = jnp.dot(both, k_im, precision=highest, preferred_element_type=jnp.float32)
        o_re = looks[b : b + beams] - (by_re[:beams] + by_im[beams:])
        o_im = looks[b + beams : b + 2 * beams] - (by_re[beams:] - by_im[:beams])
        lost = jnp.sum(b_re * y_re + b_im * y_im, axis=1, keepdims=True)
        response = (norms[b : b + beams] - lost) / loading_level
        scale = 1.0 / (loading_level * jnp.sqrt(response))
        for part, o in enumerate((o_re, o_im)):
            o = o * scale
            mine = o[:, :gate_dev]
            for r in range(1, rngs):
                mine = jnp.where(place == r, o[:, r * gate_dev : (r + 1) * gate_dev], mine)
            out_ref[part, k] = mine


def steering_rows(steer_index, dops, slot):
    bin_dev, beams = steer_index.shape
    steering = jnp.transpose(steering_table(steer_index), (0, 2, 1))
    cosine = steering[:, :, :ELEMENTS].reshape(bin_dev, beams, dops, 1, slot)
    sine_part = steering[:, :, ELEMENTS:].reshape(bin_dev, beams, dops, 1, slot)
    real_rows = jnp.concatenate([cosine, sine_part], axis=3)
    imag_rows = jnp.concatenate([-sine_part, cosine], axis=3)
    rows = jnp.stack([real_rows, imag_rows], axis=1)
    own = jnp.eye(bin_dev, dtype=jnp.float32)[:, None, None, None, :, None, None]
    return (rows[:, :, :, :, None] * own).reshape(2 * bin_dev * beams, dops * LANES)


def adapt(rows, range_code, steer, gate_dev, bin_dev):
    dops, rngs = rows.shape[0] - 1, rows.shape[1]
    gates = gate_dev * rngs
    beams = steer.shape[0] // (2 * bin_dev)
    vmem = pl.BlockSpec(memory_space=pltpu.VMEM)
    return pl.pallas_call(
        lambda *refs: adapt_kernel(gate_dev, bin_dev, *refs),
        in_specs=[pl.BlockSpec(memory_space=pltpu.SMEM), vmem, vmem],
        out_specs=vmem,
        out_shape=jax.ShapeDtypeStruct((2, bin_dev, beams, gate_dev), jnp.float32),
        scratch_shapes=[pltpu.VMEM((dops, gates + 16, LANES), jnp.float32)] * 2,
        compiler_params=pltpu.CompilerParams(vmem_limit_bytes=32 * 1024 * 1024),
    )(range_code, steer, rows)


def dual_shards(raw_samples, filter_taps, range_code, train_mask, steer_index):
    elem_dev, gate_dev = raw_samples.shape[:2]
    bin_dev = train_mask.shape[0]
    dops, rngs = lax.axis_size("dop"), lax.axis_size("rng")
    rows = -(-gate_dev // 16) * 16
    spectra = channelize(raw_samples, filter_taps, bin_dev * dops, dops, rows)
    mask_rows = jnp.repeat(jnp.transpose(train_mask), LANES // bin_dev, axis=1)
    mask_rows = jnp.pad(mask_rows.astype(jnp.bfloat16), ((0, rows - gate_dev), (0, 0)))
    gathered = exchange(spectra, mask_rows, dops, rngs)
    steer = steering_rows(steer_index, dops, elem_dev)
    return adapt(gathered, range_code, steer, gate_dev, bin_dev)


def shards(raw_samples, filter_taps, range_code, train_mask, steer_index):
    elem_dev, gate_dev = raw_samples.shape[:2]
    dops, rngs = lax.axis_size("dop"), lax.axis_size("rng")
    fits = (
        2 * train_mask.shape[0] * elem_dev == LANES
        and dops == 8
        and gate_dev % 8 == 0
        and gate_dev * rngs <= LANES
    )
    path = dual_shards if fits else plain_shards
    return path(raw_samples, filter_taps, range_code, train_mask, steer_index)


def solution(mesh):
    return jax.shard_map(
        shards,
        mesh=mesh,
        in_specs=(P("dop", "rng", None, None), P(), P(), P("dop", "rng"), P("dop", None)),
        out_specs=P(None, "dop", None, "rng"),
        check_vma=False,
    )
```

```python
import math

import jax
import jax.numpy as jnp
import ml_dtypes
import numpy as np
from jax import lax
from jax.experimental import pallas as pl
from jax.experimental.pallas import tpu as pltpu
from jax.sharding import PartitionSpec as P

ELEMENTS = 256
CHANNELS = 512
TAPS = 8
CODE_REACH = 3


loading_level = 0.25


def padded_2(x, sides, width):
    for axis, dim in sides:
        count, length = (lax.axis_size(axis), x.shape[dim])
        up = [(i, (i + 1) % count) for i in range(count - 1)]
        down = [(j, i) for i, j in up]
        last = lax.slice_in_dim(x, length - width, length, axis=dim)
        leading = lax.slice_in_dim(x, 0, width, axis=dim)
        before = lax.ppermute(last, axis, up)
        after = lax.ppermute(leading, axis, down)
        x = jnp.concatenate([before, x, after], axis=dim)
    return x


def dft_table(bin_total):
    mode_index = jnp.arange(CHANNELS, dtype=jnp.int32)
    bin_index = jnp.arange(bin_total, dtype=jnp.int32)
    turn_count = jnp.mod(mode_index[:, None] * bin_index[None, :], CHANNELS).astype(jnp.float32)
    phases = turn_count * (2.0 * math.pi / CHANNELS)
    cosine = jnp.cos(phases) / math.sqrt(CHANNELS)
    sine_part = jnp.sin(phases) / math.sqrt(CHANNELS)
    top_half = jnp.concatenate([cosine, -sine_part], axis=1)
    low_half = jnp.concatenate([sine_part, cosine], axis=1)
    return jnp.concatenate([top_half, low_half], axis=0).astype(jnp.bfloat16)


def compress(padded, range_code):
    gate_count = padded.shape[1] - 2 * CODE_REACH
    shape_out = (padded.shape[0], gate_count, padded.shape[3])
    real_sum = jnp.zeros(shape_out, jnp.float32)
    imag_sum = jnp.zeros(shape_out, jnp.float32)
    for offset in range(2 * CODE_REACH + 1):
        window = lax.slice_in_dim(padded, offset, offset + gate_count, axis=1).astype(jnp.float32)
        real_sum = (
            real_sum
            + range_code[0, offset] * window[:, :, 0]
            - range_code[1, offset] * window[:, :, 1]
        )
        imag_sum = (
            imag_sum
            + range_code[0, offset] * window[:, :, 1]
            + range_code[1, offset] * window[:, :, 0]
        )
    return jnp.stack([real_sum, imag_sum], axis=2).astype(jnp.bfloat16)


def local_gram(masked):
    real_rows = masked[:, :, 0]
    imag_rows = masked[:, :, 1]
    top_rows = jnp.concatenate([real_rows, imag_rows], axis=2)
    low_rows = jnp.concatenate([-imag_rows, real_rows], axis=2)
    stacked = jnp.concatenate([top_rows, low_rows], axis=1)
    return jnp.einsum("bri,brj->bij", stacked, stacked, preferred_element_type=jnp.float32)


def steering_table(steer_rows):
    element = jnp.arange(ELEMENTS, dtype=jnp.int32)
    turn_count = jnp.mod(
        element[None, :, None] * (2 * steer_rows[:, None, :] - ELEMENTS), 2 * ELEMENTS
    ).astype(jnp.float32)
    phases = turn_count * (math.pi / ELEMENTS)
    return jnp.concatenate([jnp.cos(phases), jnp.sin(phases)], axis=1)


def solve_all(factor, steering):
    return jax.vmap(
        lambda lower_part, target: jax.scipy.linalg.cho_solve((lower_part, True), target)
    )(factor, steering)


def beam_output(compressed, weights, steering):
    response = jnp.sum(steering * weights, axis=1)
    signal = compressed.astype(jnp.float32)
    weight_real = weights[:, :ELEMENTS]
    weight_imag = weights[:, ELEMENTS:]
    highest = lax.Precision.HIGHEST
    out_real = jnp.einsum(
        "bik,bgi->bkg", weight_real, signal[:, :, 0], precision=highest
    ) + jnp.einsum("bik,bgi->bkg", weight_imag, signal[:, :, 1], precision=highest)
    out_imag = jnp.einsum(
        "bik,bgi->bkg", weight_real, signal[:, :, 1], precision=highest
    ) - jnp.einsum("bik,bgi->bkg", weight_imag, signal[:, :, 0], precision=highest)
    return jnp.stack([out_real, out_imag], axis=0) / jnp.sqrt(response)[None, :, :, None]


def plain_shards(raw_samples, filter_taps, range_code, train_mask, steer_index):
    elem_dev = raw_samples.shape[0]
    gate_dev = raw_samples.shape[1]
    bin_dev = train_mask.shape[0]
    bin_total = bin_dev * lax.axis_size("dop")
    gates_total = gate_dev * lax.axis_size("rng")
    table = dft_table(bin_total)
    folded = raw_samples.astype(jnp.float32).reshape(elem_dev, gate_dev, 2, TAPS, CHANNELS)
    filtered = jnp.sum(folded * filter_taps, axis=3).astype(jnp.bfloat16)
    spectra = jnp.dot(
        filtered.reshape(elem_dev * gate_dev, 2 * CHANNELS),
        table,
        preferred_element_type=jnp.float32,
    )
    spectra = jnp.transpose(
        spectra.astype(jnp.bfloat16).reshape(elem_dev, gate_dev, 2, bin_total), (3, 1, 2, 0)
    )
    turned = lax.all_to_all(spectra, "dop", split_axis=0, concat_axis=3, tiled=True)
    padded = padded_2(turned, (("rng", 1),), CODE_REACH)
    compressed = compress(padded, range_code)
    masked = compressed * train_mask.astype(jnp.bfloat16)[:, :, None, None]
    dof_count = 2 * ELEMENTS
    identity = jnp.eye(dof_count, dtype=jnp.float32)
    steering = steering_table(steer_index)
    range_count = lax.axis_size("rng")
    owned_count = (bin_dev + range_count - 1) // range_count
    padded_bins = owned_count * range_count
    filled = jnp.pad(masked, ((0, padded_bins - bin_dev), (0, 0), (0, 0), (0, 0)))
    owned_rows = lax.all_to_all(filled, "rng", split_axis=0, concat_axis=1, tiled=True)
    owned_gram = local_gram(owned_rows) / gates_total + loading_level * identity
    owned_factor = jnp.linalg.cholesky(owned_gram)
    steer_filled = jnp.pad(steer_index, ((0, padded_bins - bin_dev), (0, 0)))
    first_bin = lax.axis_index("rng") * owned_count
    owned_steer = lax.dynamic_slice_in_dim(steer_filled, first_bin, owned_count, 0)
    owned_weights = solve_all(owned_factor, steering_table(owned_steer))
    weights = lax.all_gather(owned_weights, "rng", axis=0, tiled=True)[:bin_dev]
    return beam_output(compressed, weights, steering)


LANES = 128
MESH = pl.DeviceIdType.MESH
NT = (((1,), (1,)), ((), ()))


def pair_swapped(x, lane, slot):
    imag = jnp.mod(lane // slot, 2) == 1
    return jnp.where(imag, pltpu.roll(x, slot, 1), -pltpu.roll(x, LANES - slot, 1))


def channelize_kernel(raw_ref, taps_ref, table_ref, mask_ref, out_ref, filt_ref, spec_ref):
    elems, gates = raw_ref.shape[0], raw_ref.shape[1]
    dops, rows = out_ref.shape[0] - 1, out_ref.shape[1]
    step, steps = pl.program_id(0), pl.num_programs(0)
    taps = []
    for t in range(TAPS):
        quarters = [
            jnp.broadcast_to(taps_ref[t : t + 1, i : i + LANES], (2, LANES))
            for i in range(0, CHANNELS, LANES)
        ]
        taps.append(jnp.concatenate(quarters, axis=0))
    for gate in range(gates):

        def one(e, carry, gate=gate):
            x = raw_ref[e, gate].astype(jnp.float32)
            terms = [x[8 * t : 8 * t + 8] * taps[t] for t in range(TAPS)]
            while len(terms) > 1:
                terms = [a + b for a, b in zip(terms[::2], terms[1::2])]
            at = pl.multiple_of((gate * elems + e) * 8, 8)
            filt_ref[pl.ds(at, 8), :] = terms[0]
            return carry

        lax.fori_loop(0, elems, one, 0, unroll=8)
    parts = [
        filt_ref[pl.ds(i, gates * elems, stride=8), :].astype(jnp.bfloat16) for i in range(8)
    ]
    chunk = lax.dot_general(
        table_ref[...], jnp.concatenate(parts, axis=1), NT, preferred_element_type=jnp.float32
    )
    lane = lax.broadcasted_iota(jnp.int32, (dops, LANES), 1)
    for q in range(gates):
        row = jnp.zeros((dops, LANES), jnp.float32)
        for c in range(LANES // elems):
            piece = chunk[c * dops : (c + 1) * dops]
            shift = ((c - q) * elems) % LANES
            if shift:
                piece = pltpu.roll(piece, shift, 1)
            row = jnp.where(lane // elems == c, piece, row)
        at = pl.multiple_of((step * gates + q) * dops, 8)
        spec_ref[pl.ds(at, dops), :] = row

    @pl.when(step == steps - 1)
    def _():
        full = steps * gates
        if rows > full:
            spec_ref[pl.ds(full * dops, (rows - full) * dops), :] = jnp.zeros(
                ((rows - full) * dops, LANES), jnp.float32
            )
        for d in range(dops):
            out_ref[d] = spec_ref[pl.ds(d, rows, stride=dops), :].astype(jnp.bfloat16)
        bins, own = mask_ref.shape
        held = mask_ref[...].astype(jnp.float32)
        lane = lax.broadcasted_iota(jnp.int32, (bins, LANES), 1)
        bin_row = lax.broadcasted_iota(jnp.int32, (bins, LANES), 0)
        spread = jnp.where(lane // (LANES // bins) == bin_row, 1.0, 0.0)
        column = lax.dot_general(
            held, spread, (((0,), (0,)), ((), ())), preferred_element_type=jnp.float32
        )
        column = jnp.concatenate([column, jnp.zeros((rows - own, LANES), jnp.float32)], axis=0)
        out_ref[dops] = column.astype(jnp.bfloat16)


def constant_table(bin_total):
    mode_index, bin_index = np.arange(CHANNELS), np.arange(bin_total)
    turn_count = np.mod(mode_index[:, None] * bin_index[None, :], CHANNELS).astype(np.float32)
    phases = turn_count * np.float32(2.0 * math.pi / CHANNELS)
    cosine = np.cos(phases) / np.float32(math.sqrt(CHANNELS))
    sine_part = np.sin(phases) / np.float32(math.sqrt(CHANNELS))
    table = np.block([[cosine, -sine_part], [sine_part, cosine]])
    return table.astype(ml_dtypes.bfloat16)


def channelize(raw, filter_taps, train_mask, bin_total, dops, rows):
    elems, gates = raw.shape[0], raw.shape[1]
    bin_dev = bin_total // dops
    quarters = CHANNELS // LANES
    view = raw.reshape(elems, gates, 2, TAPS * quarters, LANES)
    view = jnp.transpose(view, (0, 1, 3, 2, 4)).reshape(elems, gates, 2 * TAPS * quarters, LANES)
    table = constant_table(bin_total).reshape(2, quarters, LANES, 2, dops, bin_dev)
    table = jnp.asarray(
        np.transpose(table, (5, 3, 4, 1, 0, 2)).reshape(2 * bin_total, 2 * CHANNELS)
    )
    block = LANES // elems
    return pl.pallas_call(
        channelize_kernel,
        grid=(gates // block,),
        in_specs=[
            pl.BlockSpec((elems, block, 2 * TAPS * quarters, LANES), lambda i: (0, i, 0, 0)),
            pl.BlockSpec(filter_taps.shape, lambda i: (0, 0)),
            pl.BlockSpec(table.shape, lambda i: (0, 0)),
            pl.BlockSpec(train_mask.shape, lambda i: (0, 0)),
        ],
        out_specs=pl.BlockSpec((dops + 1, rows, LANES), lambda i: (0, 0, 0)),
        out_shape=jax.ShapeDtypeStruct((dops + 1, rows, LANES), jnp.bfloat16),
        scratch_shapes=[
            pltpu.VMEM((elems * block * 8, LANES), jnp.float32),
            pltpu.VMEM((rows * dops, LANES), jnp.float32),
        ],
        compiler_params=pltpu.CompilerParams(vmem_limit_bytes=56 * 1024 * 1024),
    )(view, filter_taps, table, train_mask)


def exchange_kernel(dops, rngs, spec_ref, out_ref, send1, recv1, send2, recv2):
    d, r = lax.axis_index("dop"), lax.axis_index("rng")
    barrier = pltpu.get_barrier_semaphore()
    for i in range(1, dops):
        pl.semaphore_signal(
            barrier, inc=1, device_id=(lax.rem(d + i, dops), r), device_id_type=MESH
        )
    for j in range(1, rngs):
        pl.semaphore_signal(
            barrier, inc=1, device_id=(d, lax.rem(r + j, rngs)), device_id_type=MESH
        )
    pl.semaphore_wait(barrier, dops + rngs - 2)
    turns = []
    for i in range(1, dops):
        to = lax.rem(d + i, dops)
        turns.append(
            pltpu.make_async_remote_copy(
                src_ref=spec_ref.at[to],
                dst_ref=out_ref.at[r, d],
                send_sem=send1.at[i],
                recv_sem=recv1.at[i],
                device_id=(to, r),
                device_id_type=MESH,
            )
        )
        turns[-1].start()
    out_ref[r, d] = spec_ref[d]
    out_ref[r, dops] = spec_ref[dops]
    for copy in turns:
        copy.wait_recv()
    passed = []
    for j in range(1, rngs):
        copy = pltpu.make_async_remote_copy(
            src_ref=out_ref.at[r],
            dst_ref=out_ref.at[r],
            send_sem=send2.at[j],
            recv_sem=recv2.at[j],
            device_id=(d, lax.rem(r + j, rngs)),
            device_id_type=MESH,
        )
        copy.start()
        passed.append(copy)
    for copy in passed:
        copy.wait_recv()
    for copy in turns + passed:
        copy.wait_send()


def exchange(spectra, rngs):
    dops = spectra.shape[0] - 1
    return pl.pallas_call(
        lambda *refs: exchange_kernel(dops, rngs, *refs),
        in_specs=[pl.BlockSpec(memory_space=pltpu.VMEM)],
        out_specs=pl.BlockSpec(memory_space=pltpu.VMEM),
        out_shape=jax.ShapeDtypeStruct((rngs,) + spectra.shape, jnp.bfloat16),
        scratch_shapes=[
            pltpu.SemaphoreType.DMA((dops,)),
            pltpu.SemaphoreType.DMA((dops,)),
            pltpu.SemaphoreType.DMA((rngs,)),
            pltpu.SemaphoreType.DMA((rngs,)),
        ],
        compiler_params=pltpu.CompilerParams(collective_id=0, has_side_effects=True),
    )(spectra)


def eliminate(problems):
    states = []
    for a_re, a_im, b_re, b_im in problems:
        size = a_re.shape[0]
        tiles = [
            [a_re[i : i + 8], a_im[i : i + 8]] for i in range(0, size, 8)
        ] + [[b_re, b_im]]
        states.append(tiles)
    lanes = {
        rows: lax.broadcasted_iota(jnp.int32, (rows, size), 1) for rows in (1, 8, b_re.shape[0])
    }
    for p in range(0, size, 2):
        first, s = divmod(p, 8)
        for tiles in states:
            u_re, u_im = (part[s : s + 1] for part in tiles[first])
            v_re, v_im = (part[s + 1 : s + 2] for part in tiles[first])
            a, c = u_re[:, p : p + 1], v_re[:, p + 1 : p + 2]
            b_re, b_im = u_re[:, p + 1 : p + 2], u_im[:, p + 1 : p + 2]
            inverse = 1.0 / (a * c - (b_re * b_re + b_im * b_im))
            a, c, b_re, b_im = a * inverse, c * inverse, b_re * inverse, b_im * inverse
            one, two = lanes[1] == p, lanes[1] == p + 1
            pair = one | two
            u_re = jnp.where(pair, jnp.where(one, -1.0, 0.0), u_re)
            v_re = jnp.where(pair, jnp.where(two, -1.0, 0.0), v_re)
            u_im, v_im = jnp.where(pair, 0.0, u_im), jnp.where(pair, 0.0, v_im)
            f_re = c * u_re - (b_re * v_re - b_im * v_im)
            f_im = c * u_im - (b_re * v_im + b_im * v_re)
            g_re = a * v_re - (b_re * u_re + b_im * u_im)
            g_im = a * v_im - (b_re * u_im - b_im * u_re)
            begin = first + 1 if s == 6 else first
            for tile in tiles[begin:]:
                t_re, t_im = tile
                x_re, x_im = t_re[:, p : p + 1], t_im[:, p : p + 1]
                y_re, y_im = t_re[:, p + 1 : p + 2], t_im[:, p + 1 : p + 2]
                at = lanes[t_re.shape[0]]
                keep = (at != p) & (at != p + 1)
                tile[0] = jnp.where(keep, t_re, 0.0) - (
                    (x_re * f_re - x_im * f_im) + (y_re * g_re - y_im * g_im)
                )
                tile[1] = jnp.where(keep, t_im, 0.0) - (
                    (x_re * f_im + x_im * f_re) + (y_re * g_im + y_im * g_re)
                )
    return [tiles[-1] for tiles in states]


def adapt_kernel(gate_dev, bin_dev, code_ref, steer_ref, rows_ref, out_ref, self_ref, turned_ref):
    rngs, dops = rows_ref.shape[0], rows_ref.shape[1] - 1
    gates = gate_dev * rngs
    slot = LANES // (2 * bin_dev)
    lane_dev = lax.broadcasted_iota(jnp.int32, (gate_dev, LANES), 1)
    lane = lax.broadcasted_iota(jnp.int32, (gates, LANES), 1)
    mask = jnp.concatenate(
        [rows_ref[r, dops].astype(jnp.float32)[:gate_dev] for r in range(rngs)], axis=0
    )
    signal, turned, train, train_turned = [], [], [], []
    edge = jnp.zeros((8, LANES), jnp.float32)
    for d in range(dops):
        for ref in (self_ref, turned_ref):
            ref[d, 0:8] = edge
            ref[d, 8 + gates : 16 + gates] = edge
        for r in range(rngs):
            y = rows_ref[r, d].astype(jnp.float32)[:gate_dev]
            at = 8 + r * gate_dev
            self_ref[d, at : at + gate_dev] = y
            turned_ref[d, at : at + gate_dev] = pair_swapped(y, lane_dev, slot)
        total = jnp.zeros((gates, LANES), jnp.float32)
        for t in range(2 * CODE_REACH + 1):
            at = 8 - CODE_REACH + t
            total = (
                total
                + code_ref[0:1, t : t + 1] * self_ref[d, at : at + gates]
                + code_ref[1:2, t : t + 1] * turned_ref[d, at : at + gates]
            )
        v = total.astype(jnp.bfloat16).astype(jnp.float32)
        q = pair_swapped(v, lane, slot)
        signal.append(v.astype(jnp.bfloat16))
        turned.append(q.astype(jnp.bfloat16))
        train.append((v * mask).astype(jnp.bfloat16))
        train_turned.append((q * mask).astype(jnp.bfloat16))

    def dot(a, b):
        return lax.dot_general(a, b, NT, preferred_element_type=jnp.float32)

    def of_bins(parts):
        rows = []
        for k in range(bin_dev):
            own = lane // (2 * slot) == k
            rows.append(
                jnp.concatenate(
                    [jnp.where(own, x.astype(jnp.float32), 0.0).astype(jnp.bfloat16) for x in parts],
                    axis=1,
                )
            )
        return jnp.concatenate(rows, axis=0)

    signal_bins, train_bins = of_bins(signal), of_bins(train)
    signal, turned, train, train_turned = (
        jnp.concatenate(x, axis=1) for x in (signal, turned, train, train_turned)
    )
    all_re, all_im = dot(signal_bins, signal), dot(signal_bins, turned)
    gram_re, gram_im = dot(train_bins, train), dot(train_bins, train_turned)
    steer = steering_rows(steer_ref[...], dops, slot)
    high = steer.astype(jnp.bfloat16)
    rest = steer - high.astype(jnp.float32)
    middle = rest.astype(jnp.bfloat16)
    low = (rest - middle.astype(jnp.float32)).astype(jnp.bfloat16)
    looks = dot(high, signal) + (dot(middle, signal) + dot(low, signal))
    sights = dot(high, train) + (dot(middle, train) + dot(low, train))
    norms = jnp.sum(steer * steer, axis=1, keepdims=True)
    beams = steer.shape[0] // (2 * bin_dev)
    diagonal = (
        lax.broadcasted_iota(jnp.int32, (gates, gates), 0)
        == lax.broadcasted_iota(jnp.int32, (gates, gates), 1)
    )
    loading = jnp.where(diagonal, loading_level * gates, 0.0)
    problems = []
    for k in range(bin_dev):
        at, b = k * gates, 2 * k * beams
        problems.append(
            (
                gram_re[at : at + gates] + loading,
                -gram_im[at : at + gates],
                sights[b : b + beams],
                sights[b + beams : b + 2 * beams],
            )
        )
    solved = eliminate(problems)
    place = lax.axis_index("rng")
    highest = lax.Precision.HIGHEST
    for k in range(bin_dev):
        y_re, y_im = solved[k]
        b_re, b_im = problems[k][2:]
        at, b = k * gates, 2 * k * beams
        k_re, k_im = all_re[at : at + gates], all_im[at : at + gates]
        both = jnp.concatenate([y_re, y_im], axis=0)
        by_re = jnp.dot(both, k_re, precision=highest, preferred_element_type=jnp.float32)
        by_im = jnp.dot(both, k_im, precision=highest, preferred_element_type=jnp.float32)
        o_re = looks[b : b + beams] - (by_re[:beams] + by_im[beams:])
        o_im = looks[b + beams : b + 2 * beams] - (by_re[beams:] - by_im[:beams])
        lost = jnp.sum(b_re * y_re + b_im * y_im, axis=1, keepdims=True)
        response = (norms[b : b + beams] - lost) / loading_level
        scale = 1.0 / (loading_level * jnp.sqrt(response))
        for part, o in enumerate((o_re, o_im)):
            o = o * scale
            mine = o[:, :gate_dev]
            for r in range(1, rngs):
                mine = jnp.where(place == r, o[:, r * gate_dev : (r + 1) * gate_dev], mine)
            out_ref[part, k] = mine


def steering_rows(steer_index, dops, slot):
    bins, beams = steer_index.shape
    looks = [
        jnp.broadcast_to(steer_index[k : k + 1, j : j + 1], (1, LANES))
        for k in range(bins)
        for _ in range(2)
        for j in range(beams)
    ]
    look = 2 * jnp.concatenate(looks, axis=0) - ELEMENTS
    lane = lax.broadcasted_iota(jnp.int32, look.shape, 1)
    row = lax.broadcasted_iota(jnp.int32, look.shape, 0)
    own = lane // (2 * slot) == row // (2 * beams)
    quarter = (ELEMENTS // 2) * ((row // beams) % 2 - (lane // slot) % 2)
    parts = []
    for d in range(dops):
        element = d * slot + lane % slot
        turn = jnp.bitwise_and(element * look + quarter, 2 * ELEMENTS - 1)
        turn = jnp.where(turn >= ELEMENTS, turn - 2 * ELEMENTS, turn)
        value = jnp.cos(turn.astype(jnp.float32) * (math.pi / ELEMENTS))
        parts.append(jnp.where(own, value, 0.0))
    return jnp.concatenate(parts, axis=1)


def adapt(rows, range_code, steer, gate_dev, bin_dev):
    rngs, dops = rows.shape[0], rows.shape[1] - 1
    gates = gate_dev * rngs
    beams = steer.shape[1]
    vmem = pl.BlockSpec(memory_space=pltpu.VMEM)
    return pl.pallas_call(
        lambda *refs: adapt_kernel(gate_dev, bin_dev, *refs),
        in_specs=[vmem, vmem, vmem],
        out_specs=vmem,
        out_shape=jax.ShapeDtypeStruct((2, bin_dev, beams, gate_dev), jnp.float32),
        scratch_shapes=[pltpu.VMEM((dops, gates + 16, LANES), jnp.float32)] * 2,
        compiler_params=pltpu.CompilerParams(vmem_limit_bytes=32 * 1024 * 1024),
    )(range_code, steer, rows)


def dual_shards(raw_samples, filter_taps, range_code, train_mask, steer_index):
    elem_dev, gate_dev = raw_samples.shape[:2]
    bin_dev = train_mask.shape[0]
    dops, rngs = lax.axis_size("dop"), lax.axis_size("rng")
    rows = -(-gate_dev // 16) * 16
    spectra = channelize(raw_samples, filter_taps, train_mask, bin_dev * dops, dops, rows)
    gathered = exchange(spectra, rngs)
    return adapt(gathered, range_code, steer_index, gate_dev, bin_dev)


def shards(raw_samples, filter_taps, range_code, train_mask, steer_index):
    elem_dev, gate_dev = raw_samples.shape[:2]
    dops, rngs = lax.axis_size("dop"), lax.axis_size("rng")
    fits = (
        2 * train_mask.shape[0] * elem_dev == LANES
        and dops == 8
        and gate_dev % 8 == 0
        and gate_dev * rngs <= LANES
    )
    path = dual_shards if fits else plain_shards
    return path(raw_samples, filter_taps, range_code, train_mask, steer_index)


def solution(mesh):
    return jax.shard_map(
        shards,
        mesh=mesh,
        in_specs=(P("dop", "rng", None, None), P(), P(), P("dop", "rng"), P("dop", None)),
        out_specs=P(None, "dop", None, "rng"),
        check_vma=False,
    )
```

```python
import math

import jax
import jax.numpy as jnp
import ml_dtypes
import numpy as np
from jax import lax
from jax.experimental import pallas as pl
from jax.experimental.pallas import tpu as pltpu
from jax.sharding import PartitionSpec as P

ELEMENTS = 256
CHANNELS = 512
TAPS = 8
CODE_REACH = 3


loading_level = 0.25


def padded_2(x, sides, width):
    for axis, dim in sides:
        count, length = (lax.axis_size(axis), x.shape[dim])
        up = [(i, (i + 1) % count) for i in range(count - 1)]
        down = [(j, i) for i, j in up]
        last = lax.slice_in_dim(x, length - width, length, axis=dim)
        leading = lax.slice_in_dim(x, 0, width, axis=dim)
        before = lax.ppermute(last, axis, up)
        after = lax.ppermute(leading, axis, down)
        x = jnp.concatenate([before, x, after], axis=dim)
    return x


def dft_table(bin_total):
    mode_index = jnp.arange(CHANNELS, dtype=jnp.int32)
    bin_index = jnp.arange(bin_total, dtype=jnp.int32)
    turn_count = jnp.mod(mode_index[:, None] * bin_index[None, :], CHANNELS).astype(jnp.float32)
    phases = turn_count * (2.0 * math.pi / CHANNELS)
    cosine = jnp.cos(phases) / math.sqrt(CHANNELS)
    sine_part = jnp.sin(phases) / math.sqrt(CHANNELS)
    top_half = jnp.concatenate([cosine, -sine_part], axis=1)
    low_half = jnp.concatenate([sine_part, cosine], axis=1)
    return jnp.concatenate([top_half, low_half], axis=0).astype(jnp.bfloat16)


def compress(padded, range_code):
    gate_count = padded.shape[1] - 2 * CODE_REACH
    shape_out = (padded.shape[0], gate_count, padded.shape[3])
    real_sum = jnp.zeros(shape_out, jnp.float32)
    imag_sum = jnp.zeros(shape_out, jnp.float32)
    for offset in range(2 * CODE_REACH + 1):
        window = lax.slice_in_dim(padded, offset, offset + gate_count, axis=1).astype(jnp.float32)
        real_sum = (
            real_sum
            + range_code[0, offset] * window[:, :, 0]
            - range_code[1, offset] * window[:, :, 1]
        )
        imag_sum = (
            imag_sum
            + range_code[0, offset] * window[:, :, 1]
            + range_code[1, offset] * window[:, :, 0]
        )
    return jnp.stack([real_sum, imag_sum], axis=2).astype(jnp.bfloat16)


def local_gram(masked):
    real_rows = masked[:, :, 0]
    imag_rows = masked[:, :, 1]
    top_rows = jnp.concatenate([real_rows, imag_rows], axis=2)
    low_rows = jnp.concatenate([-imag_rows, real_rows], axis=2)
    stacked = jnp.concatenate([top_rows, low_rows], axis=1)
    return jnp.einsum("bri,brj->bij", stacked, stacked, preferred_element_type=jnp.float32)


def steering_table(steer_rows):
    element = jnp.arange(ELEMENTS, dtype=jnp.int32)
    turn_count = jnp.mod(
        element[None, :, None] * (2 * steer_rows[:, None, :] - ELEMENTS), 2 * ELEMENTS
    ).astype(jnp.float32)
    phases = turn_count * (math.pi / ELEMENTS)
    return jnp.concatenate([jnp.cos(phases), jnp.sin(phases)], axis=1)


def solve_all(factor, steering):
    return jax.vmap(
        lambda lower_part, target: jax.scipy.linalg.cho_solve((lower_part, True), target)
    )(factor, steering)


def beam_output(compressed, weights, steering):
    response = jnp.sum(steering * weights, axis=1)
    signal = compressed.astype(jnp.float32)
    weight_real = weights[:, :ELEMENTS]
    weight_imag = weights[:, ELEMENTS:]
    highest = lax.Precision.HIGHEST
    out_real = jnp.einsum(
        "bik,bgi->bkg", weight_real, signal[:, :, 0], precision=highest
    ) + jnp.einsum("bik,bgi->bkg", weight_imag, signal[:, :, 1], precision=highest)
    out_imag = jnp.einsum(
        "bik,bgi->bkg", weight_real, signal[:, :, 1], precision=highest
    ) - jnp.einsum("bik,bgi->bkg", weight_imag, signal[:, :, 0], precision=highest)
    return jnp.stack([out_real, out_imag], axis=0) / jnp.sqrt(response)[None, :, :, None]


def plain_shards(raw_samples, filter_taps, range_code, train_mask, steer_index):
    elem_dev = raw_samples.shape[0]
    gate_dev = raw_samples.shape[1]
    bin_dev = train_mask.shape[0]
    bin_total = bin_dev * lax.axis_size("dop")
    gates_total = gate_dev * lax.axis_size("rng")
    table = dft_table(bin_total)
    folded = raw_samples.astype(jnp.float32).reshape(elem_dev, gate_dev, 2, TAPS, CHANNELS)
    filtered = jnp.sum(folded * filter_taps, axis=3).astype(jnp.bfloat16)
    spectra = jnp.dot(
        filtered.reshape(elem_dev * gate_dev, 2 * CHANNELS),
        table,
        preferred_element_type=jnp.float32,
    )
    spectra = jnp.transpose(
        spectra.astype(jnp.bfloat16).reshape(elem_dev, gate_dev, 2, bin_total), (3, 1, 2, 0)
    )
    turned = lax.all_to_all(spectra, "dop", split_axis=0, concat_axis=3, tiled=True)
    padded = padded_2(turned, (("rng", 1),), CODE_REACH)
    compressed = compress(padded, range_code)
    masked = compressed * train_mask.astype(jnp.bfloat16)[:, :, None, None]
    dof_count = 2 * ELEMENTS
    identity = jnp.eye(dof_count, dtype=jnp.float32)
    steering = steering_table(steer_index)
    range_count = lax.axis_size("rng")
    owned_count = (bin_dev + range_count - 1) // range_count
    padded_bins = owned_count * range_count
    filled = jnp.pad(masked, ((0, padded_bins - bin_dev), (0, 0), (0, 0), (0, 0)))
    owned_rows = lax.all_to_all(filled, "rng", split_axis=0, concat_axis=1, tiled=True)
    owned_gram = local_gram(owned_rows) / gates_total + loading_level * identity
    owned_factor = jnp.linalg.cholesky(owned_gram)
    steer_filled = jnp.pad(steer_index, ((0, padded_bins - bin_dev), (0, 0)))
    first_bin = lax.axis_index("rng") * owned_count
    owned_steer = lax.dynamic_slice_in_dim(steer_filled, first_bin, owned_count, 0)
    owned_weights = solve_all(owned_factor, steering_table(owned_steer))
    weights = lax.all_gather(owned_weights, "rng", axis=0, tiled=True)[:bin_dev]
    return beam_output(compressed, weights, steering)


LANES = 128
MESH = pl.DeviceIdType.MESH
NT = (((1,), (1,)), ((), ()))


def pair_swapped(x, lane, slot):
    imag = jnp.mod(lane // slot, 2) == 1
    return jnp.where(imag, pltpu.roll(x, slot, 1), -pltpu.roll(x, LANES - slot, 1))


def channelize_kernel(raw_ref, taps_ref, table_ref, mask_ref, out_ref, filt_ref, spec_ref):
    elems, gates = raw_ref.shape[0], raw_ref.shape[1]
    dops, rows = out_ref.shape[0] - 1, out_ref.shape[1]
    step, steps = pl.program_id(0), pl.num_programs(0)
    taps = []
    for t in range(TAPS):
        quarters = [
            jnp.broadcast_to(taps_ref[t : t + 1, i : i + LANES], (2, LANES))
            for i in range(0, CHANNELS, LANES)
        ]
        taps.append(jnp.concatenate(quarters, axis=0))
    for gate in range(gates):

        def one(e, carry, gate=gate):
            x = raw_ref[e, gate].astype(jnp.float32)
            terms = [x[8 * t : 8 * t + 8] * taps[t] for t in range(TAPS)]
            while len(terms) > 1:
                terms = [a + b for a, b in zip(terms[::2], terms[1::2])]
            at = pl.multiple_of((gate * elems + e) * 8, 8)
            filt_ref[pl.ds(at, 8), :] = terms[0]
            return carry

        lax.fori_loop(0, elems, one, 0, unroll=8)
    parts = [
        filt_ref[pl.ds(i, gates * elems, stride=8), :].astype(jnp.bfloat16) for i in range(8)
    ]
    chunk = jnp.dot(
        jnp.concatenate(parts, axis=1), table_ref[...], preferred_element_type=jnp.float32
    )
    chunk = jnp.transpose(chunk)
    lane = lax.broadcasted_iota(jnp.int32, (dops, LANES), 1)
    for q in range(gates):
        row = jnp.zeros((dops, LANES), jnp.float32)
        for c in range(LANES // elems):
            piece = chunk[c * dops : (c + 1) * dops]
            shift = ((c - q) * elems) % LANES
            if shift:
                piece = pltpu.roll(piece, shift, 1)
            row = jnp.where(lane // elems == c, piece, row)
        at = pl.multiple_of((step * gates + q) * dops, 8)
        spec_ref[pl.ds(at, dops), :] = row

    @pl.when(step == steps - 1)
    def _():
        full = steps * gates
        if rows > full:
            spec_ref[pl.ds(full * dops, (rows - full) * dops), :] = jnp.zeros(
                ((rows - full) * dops, LANES), jnp.float32
            )
        for d in range(dops):
            out_ref[d] = spec_ref[pl.ds(d, rows, stride=dops), :].astype(jnp.bfloat16)
        bins, own = mask_ref.shape
        held = mask_ref[...].astype(jnp.float32)
        lane = lax.broadcasted_iota(jnp.int32, (bins, LANES), 1)
        bin_row = lax.broadcasted_iota(jnp.int32, (bins, LANES), 0)
        spread = jnp.where(lane // (LANES // bins) == bin_row, 1.0, 0.0)
        column = lax.dot_general(
            held, spread, (((0,), (0,)), ((), ())), preferred_element_type=jnp.float32
        )
        column = jnp.concatenate([column, jnp.zeros((rows - own, LANES), jnp.float32)], axis=0)
        out_ref[dops] = column.astype(jnp.bfloat16)


def constant_table(bin_total):
    mode_index, bin_index = np.arange(CHANNELS), np.arange(bin_total)
    turn_count = np.mod(mode_index[:, None] * bin_index[None, :], CHANNELS).astype(np.float32)
    phases = turn_count * np.float32(2.0 * math.pi / CHANNELS)
    cosine = np.cos(phases) / np.float32(math.sqrt(CHANNELS))
    sine_part = np.sin(phases) / np.float32(math.sqrt(CHANNELS))
    table = np.block([[cosine, -sine_part], [sine_part, cosine]])
    return table.astype(ml_dtypes.bfloat16)


def channelize(raw, filter_taps, train_mask, bin_total, dops, rows):
    elems, gates = raw.shape[0], raw.shape[1]
    bin_dev = bin_total // dops
    quarters = CHANNELS // LANES
    view = raw.reshape(elems, gates, 2, TAPS * quarters, LANES)
    view = jnp.transpose(view, (0, 1, 3, 2, 4)).reshape(elems, gates, 2 * TAPS * quarters, LANES)
    table = constant_table(bin_total).reshape(2, quarters, LANES, 2, dops, bin_dev)
    table = jnp.asarray(
        np.pad(
            np.transpose(table, (1, 0, 2, 5, 3, 4)).reshape(2 * CHANNELS, 2 * bin_total),
            ((0, 0), (0, LANES - 2 * bin_total)),
        )
    )
    block = LANES // elems
    return pl.pallas_call(
        channelize_kernel,
        grid=(gates // block,),
        in_specs=[
            pl.BlockSpec((elems, block, 2 * TAPS * quarters, LANES), lambda i: (0, i, 0, 0)),
            pl.BlockSpec(filter_taps.shape, lambda i: (0, 0)),
            pl.BlockSpec(table.shape, lambda i: (0, 0)),
            pl.BlockSpec(train_mask.shape, lambda i: (0, 0)),
        ],
        out_specs=pl.BlockSpec((dops + 1, rows, LANES), lambda i: (0, 0, 0)),
        out_shape=jax.ShapeDtypeStruct((dops + 1, rows, LANES), jnp.bfloat16),
        scratch_shapes=[
            pltpu.VMEM((elems * block * 8, LANES), jnp.float32),
            pltpu.VMEM((rows * dops, LANES), jnp.float32),
        ],
        compiler_params=pltpu.CompilerParams(vmem_limit_bytes=56 * 1024 * 1024),
    )(view, filter_taps, table, train_mask)


def exchange_kernel(dops, rngs, spec_ref, out_ref, send1, recv1, send2, recv2):
    d, r = lax.axis_index("dop"), lax.axis_index("rng")
    barrier = pltpu.get_barrier_semaphore()
    for i in range(1, dops):
        pl.semaphore_signal(
            barrier, inc=1, device_id=(lax.rem(d + i, dops), r), device_id_type=MESH
        )
    for j in range(1, rngs):
        pl.semaphore_signal(
            barrier, inc=1, device_id=(d, lax.rem(r + j, rngs)), device_id_type=MESH
        )
    pl.semaphore_wait(barrier, dops + rngs - 2)
    turns = []
    for i in range(1, dops):
        to = lax.rem(d + i, dops)
        turns.append(
            pltpu.make_async_remote_copy(
                src_ref=spec_ref.at[to],
                dst_ref=out_ref.at[r, d],
                send_sem=send1.at[i],
                recv_sem=recv1.at[i],
                device_id=(to, r),
                device_id_type=MESH,
            )
        )
        turns[-1].start()
    out_ref[r, d] = spec_ref[d]
    out_ref[r, dops] = spec_ref[dops]
    for copy in turns:
        copy.wait_recv()
    passed = []
    for j in range(1, rngs):
        copy = pltpu.make_async_remote_copy(
            src_ref=out_ref.at[r],
            dst_ref=out_ref.at[r],
            send_sem=send2.at[j],
            recv_sem=recv2.at[j],
            device_id=(d, lax.rem(r + j, rngs)),
            device_id_type=MESH,
        )
        copy.start()
        passed.append(copy)
    for copy in passed:
        copy.wait_recv()
    for copy in turns + passed:
        copy.wait_send()


def exchange(spectra, rngs):
    dops = spectra.shape[0] - 1
    return pl.pallas_call(
        lambda *refs: exchange_kernel(dops, rngs, *refs),
        in_specs=[pl.BlockSpec(memory_space=pltpu.VMEM)],
        out_specs=pl.BlockSpec(memory_space=pltpu.VMEM),
        out_shape=jax.ShapeDtypeStruct((rngs,) + spectra.shape, jnp.bfloat16),
        scratch_shapes=[
            pltpu.SemaphoreType.DMA((dops,)),
            pltpu.SemaphoreType.DMA((dops,)),
            pltpu.SemaphoreType.DMA((rngs,)),
            pltpu.SemaphoreType.DMA((rngs,)),
        ],
        compiler_params=pltpu.CompilerParams(
            collective_id=0, has_side_effects=True, vmem_limit_bytes=8 * 1024 * 1024
        ),
    )(spectra)


def eliminate(problems):
    states = []
    for a_re, a_im, b_re, b_im in problems:
        size = a_re.shape[0]
        tiles = [
            [a_re[i : i + 8], a_im[i : i + 8]] for i in range(0, size, 8)
        ] + [[b_re, b_im]]
        states.append(tiles)
    lanes = {
        rows: lax.broadcasted_iota(jnp.int32, (rows, size), 1) for rows in (1, 8, b_re.shape[0])
    }
    for p in range(0, size, 2):
        first, s = divmod(p, 8)
        for tiles in states:
            u_re, u_im = (part[s : s + 1] for part in tiles[first])
            v_re, v_im = (part[s + 1 : s + 2] for part in tiles[first])
            a, c = u_re[:, p : p + 1], v_re[:, p + 1 : p + 2]
            b_re, b_im = u_re[:, p + 1 : p + 2], u_im[:, p + 1 : p + 2]
            inverse = 1.0 / (a * c - (b_re * b_re + b_im * b_im))
            a, c, b_re, b_im = a * inverse, c * inverse, b_re * inverse, b_im * inverse
            one, two = lanes[1] == p, lanes[1] == p + 1
            pair = one | two
            u_re = jnp.where(pair, jnp.where(one, -1.0, 0.0), u_re)
            v_re = jnp.where(pair, jnp.where(two, -1.0, 0.0), v_re)
            u_im, v_im = jnp.where(pair, 0.0, u_im), jnp.where(pair, 0.0, v_im)
            f_re = c * u_re - (b_re * v_re - b_im * v_im)
            f_im = c * u_im - (b_re * v_im + b_im * v_re)
            g_re = a * v_re - (b_re * u_re + b_im * u_im)
            g_im = a * v_im - (b_re * u_im - b_im * u_re)
            begin = first + 1 if s == 6 else first
            for tile in tiles[begin:]:
                t_re, t_im = tile
                x_re, x_im = t_re[:, p : p + 1], t_im[:, p : p + 1]
                y_re, y_im = t_re[:, p + 1 : p + 2], t_im[:, p + 1 : p + 2]
                at = lanes[t_re.shape[0]]
                keep = (at != p) & (at != p + 1)
                tile[0] = jnp.where(keep, t_re, 0.0) - (
                    (x_re * f_re - x_im * f_im) + (y_re * g_re - y_im * g_im)
                )
                tile[1] = jnp.where(keep, t_im, 0.0) - (
                    (x_re * f_im + x_im * f_re) + (y_re * g_im + y_im * g_re)
                )
    return [tiles[-1] for tiles in states]


def adapt_kernel(gate_dev, bin_dev, code_ref, steer_ref, rows_ref, out_ref, self_ref, turned_ref):
    rngs, dops = rows_ref.shape[0], rows_ref.shape[1] - 1
    gates = gate_dev * rngs
    slot = LANES // (2 * bin_dev)
    lane_dev = lax.broadcasted_iota(jnp.int32, (gate_dev, LANES), 1)
    lane = lax.broadcasted_iota(jnp.int32, (gates, LANES), 1)
    chosen = lax.rem(lax.axis_index("rng"), bin_dev)
    mask = jnp.concatenate(
        [rows_ref[r, dops].astype(jnp.float32)[:gate_dev] for r in range(rngs)], axis=0
    )
    signal, turned, train, train_turned = [], [], [], []
    edge = jnp.zeros((8, LANES), jnp.float32)
    for d in range(dops):
        for ref in (self_ref, turned_ref):
            ref[d, 0:8] = edge
            ref[d, 8 + gates : 16 + gates] = edge
        for r in range(rngs):
            y = rows_ref[r, d].astype(jnp.float32)[:gate_dev]
            at = 8 + r * gate_dev
            self_ref[d, at : at + gate_dev] = y
            turned_ref[d, at : at + gate_dev] = pair_swapped(y, lane_dev, slot)
        total = jnp.zeros((gates, LANES), jnp.float32)
        for t in range(2 * CODE_REACH + 1):
            at = 8 - CODE_REACH + t
            total = (
                total
                + code_ref[0:1, t : t + 1] * self_ref[d, at : at + gates]
                + code_ref[1:2, t : t + 1] * turned_ref[d, at : at + gates]
            )
        v = total.astype(jnp.bfloat16).astype(jnp.float32)
        q = pair_swapped(v, lane, slot)
        signal.append(v.astype(jnp.bfloat16))
        turned.append(q.astype(jnp.bfloat16))
        train.append((v * mask).astype(jnp.bfloat16))
        train_turned.append((q * mask).astype(jnp.bfloat16))

    def dot(a, b):
        return lax.dot_general(a, b, NT, preferred_element_type=jnp.float32)

    own = lane // (2 * slot) == chosen

    def of_bin(parts):
        kept = [jnp.where(own, x.astype(jnp.float32), 0.0).astype(jnp.bfloat16) for x in parts]
        return jnp.concatenate(kept, axis=1)

    signal_bins, train_bins = of_bin(signal), of_bin(train)
    signal, turned, train, train_turned = (
        jnp.concatenate(x, axis=1) for x in (signal, turned, train, train_turned)
    )
    all_re, all_im = dot(signal_bins, signal), dot(signal_bins, turned)
    gram_re, gram_im = dot(train_bins, train), dot(train_bins, train_turned)
    steer = steering_rows(steer_ref[...], chosen, dops, slot)
    high = steer.astype(jnp.bfloat16)
    rest = steer - high.astype(jnp.float32)
    middle = rest.astype(jnp.bfloat16)
    low = (rest - middle.astype(jnp.float32)).astype(jnp.bfloat16)
    looks = dot(high, signal) + (dot(middle, signal) + dot(low, signal))
    sights = dot(high, train) + (dot(middle, train) + dot(low, train))
    norms = jnp.sum(steer * steer, axis=1, keepdims=True)
    beams = steer.shape[0] // 2
    diagonal = (
        lax.broadcasted_iota(jnp.int32, (gates, gates), 0)
        == lax.broadcasted_iota(jnp.int32, (gates, gates), 1)
    )
    loading = jnp.where(diagonal, loading_level * gates, 0.0)
    b_re, b_im = sights[:beams], sights[beams:]
    y_re, y_im = eliminate([(gram_re + loading, -gram_im, b_re, b_im)])[0]
    highest = lax.Precision.HIGHEST
    both = jnp.concatenate([y_re, y_im], axis=0)
    by_re = jnp.dot(both, all_re, precision=highest, preferred_element_type=jnp.float32)
    by_im = jnp.dot(both, all_im, precision=highest, preferred_element_type=jnp.float32)
    o_re = looks[:beams] - (by_re[:beams] + by_im[beams:])
    o_im = looks[beams:] - (by_re[beams:] - by_im[:beams])
    lost = jnp.sum(b_re * y_re + b_im * y_im, axis=1, keepdims=True)
    response = (norms[:beams] - lost) / loading_level
    scale = 1.0 / (loading_level * jnp.sqrt(response))
    out = jnp.concatenate([o_re * scale, o_im * scale], axis=0)
    if gates < LANES:
        out = jnp.concatenate(
            [out, jnp.zeros((2 * beams, LANES - gates), jnp.float32)], axis=1
        )
    out_ref[...] = out


def swap_kernel(gate_dev, rngs, mine_ref, out_ref, other_ref, send, recv):
    d, r = lax.axis_index("dop"), lax.axis_index("rng")
    chosen = lax.rem(r, 2)
    partner = (d, r + 1 - 2 * chosen)
    barrier = pltpu.get_barrier_semaphore()
    pl.semaphore_signal(barrier, inc=1, device_id=partner, device_id_type=MESH)
    pl.semaphore_wait(barrier, 1)
    copy = pltpu.make_async_remote_copy(
        src_ref=mine_ref,
        dst_ref=other_ref,
        send_sem=send,
        recv_sem=recv,
        device_id=partner,
        device_id_type=MESH,
    )
    copy.start()
    copy.wait()
    beams = mine_ref.shape[0] // 2

    def own_gates(x):
        out = x[:, :gate_dev]
        for i in range(1, rngs):
            out = jnp.where(r == i, x[:, i * gate_dev : (i + 1) * gate_dev], out)
        return out

    mine, other = own_gates(mine_ref[...]), own_gates(other_ref[...])
    for k in range(2):
        both = jnp.where(chosen == k, mine, other)
        for part in range(2):
            out_ref[part, k] = both[part * beams : (part + 1) * beams]


def swap(mine, gate_dev, rngs):
    vmem = pl.BlockSpec(memory_space=pltpu.VMEM)
    return pl.pallas_call(
        lambda *refs: swap_kernel(gate_dev, rngs, *refs),
        in_specs=[vmem],
        out_specs=vmem,
        out_shape=jax.ShapeDtypeStruct((2, 2, mine.shape[0] // 2, gate_dev), jnp.float32),
        scratch_shapes=[
            pltpu.VMEM(mine.shape, jnp.float32),
            pltpu.SemaphoreType.DMA,
            pltpu.SemaphoreType.DMA,
        ],
        compiler_params=pltpu.CompilerParams(
            collective_id=1, has_side_effects=True, vmem_limit_bytes=8 * 1024 * 1024
        ),
    )(mine)


def steering_rows(steer_index, chosen, dops, slot):
    bins, beams = steer_index.shape
    picked = steer_index[:1]
    for k in range(1, bins):
        picked = jnp.where(chosen == k, steer_index[k : k + 1], picked)
    looks = [jnp.broadcast_to(picked[:, j : j + 1], (1, LANES)) for j in range(beams)]
    look = 2 * jnp.concatenate(looks + looks, axis=0) - ELEMENTS
    lane = lax.broadcasted_iota(jnp.int32, look.shape, 1)
    row = lax.broadcasted_iota(jnp.int32, look.shape, 0)
    own = lane // (2 * slot) == chosen
    quarter = (ELEMENTS // 2) * (row // beams - (lane // slot) % 2)
    parts = []
    for d in range(dops):
        element = d * slot + lane % slot
        turn = jnp.bitwise_and(element * look + quarter, 2 * ELEMENTS - 1)
        turn = jnp.where(turn >= ELEMENTS, turn - 2 * ELEMENTS, turn)
        value = jnp.cos(turn.astype(jnp.float32) * (math.pi / ELEMENTS))
        parts.append(jnp.where(own, value, 0.0))
    return jnp.concatenate(parts, axis=1)


def adapt(rows, range_code, steer, gate_dev, bin_dev):
    rngs, dops = rows.shape[0], rows.shape[1] - 1
    gates = gate_dev * rngs
    beams = steer.shape[1]
    vmem = pl.BlockSpec(memory_space=pltpu.VMEM)
    return pl.pallas_call(
        lambda *refs: adapt_kernel(gate_dev, bin_dev, *refs),
        in_specs=[vmem, vmem, vmem],
        out_specs=vmem,
        out_shape=jax.ShapeDtypeStruct((2 * beams, LANES), jnp.float32),
        scratch_shapes=[pltpu.VMEM((dops, gates + 16, LANES), jnp.float32)] * 2,
        compiler_params=pltpu.CompilerParams(vmem_limit_bytes=32 * 1024 * 1024),
    )(range_code, steer, rows)


def dual_shards(raw_samples, filter_taps, range_code, train_mask, steer_index):
    elem_dev, gate_dev = raw_samples.shape[:2]
    bin_dev = train_mask.shape[0]
    dops, rngs = lax.axis_size("dop"), lax.axis_size("rng")
    rows = -(-gate_dev // 16) * 16
    spectra = channelize(raw_samples, filter_taps, train_mask, bin_dev * dops, dops, rows)
    gathered = exchange(spectra, rngs)
    mine = adapt(gathered, range_code, steer_index, gate_dev, bin_dev)
    return swap(mine, gate_dev, rngs)


def shards(raw_samples, filter_taps, range_code, train_mask, steer_index):
    elem_dev, gate_dev = raw_samples.shape[:2]
    dops, rngs = lax.axis_size("dop"), lax.axis_size("rng")
    fits = (
        2 * train_mask.shape[0] * elem_dev == LANES
        and dops == 8
        and train_mask.shape[0] == 2
        and rngs % 2 == 0
        and gate_dev % 8 == 0
        and gate_dev * rngs <= LANES
    )
    path = dual_shards if fits else plain_shards
    return path(raw_samples, filter_taps, range_code, train_mask, steer_index)


def solution(mesh):
    return jax.shard_map(
        shards,
        mesh=mesh,
        in_specs=(P("dop", "rng", None, None), P(), P(), P("dop", "rng"), P("dop", None)),
        out_specs=P(None, "dop", None, "rng"),
        check_vma=False,
    )
```

```python
import math

import jax
import jax.numpy as jnp
import ml_dtypes
import numpy as np
from jax import lax
from jax.experimental import pallas as pl
from jax.experimental.pallas import tpu as pltpu
from jax.sharding import PartitionSpec as P

ELEMENTS = 256
CHANNELS = 512
TAPS = 8
CODE_REACH = 3


loading_level = 0.25


def padded_2(x, sides, width):
    for axis, dim in sides:
        count, length = (lax.axis_size(axis), x.shape[dim])
        up = [(i, (i + 1) % count) for i in range(count - 1)]
        down = [(j, i) for i, j in up]
        last = lax.slice_in_dim(x, length - width, length, axis=dim)
        leading = lax.slice_in_dim(x, 0, width, axis=dim)
        before = lax.ppermute(last, axis, up)
        after = lax.ppermute(leading, axis, down)
        x = jnp.concatenate([before, x, after], axis=dim)
    return x


def dft_table(bin_total):
    mode_index = jnp.arange(CHANNELS, dtype=jnp.int32)
    bin_index = jnp.arange(bin_total, dtype=jnp.int32)
    turn_count = jnp.mod(mode_index[:, None] * bin_index[None, :], CHANNELS).astype(jnp.float32)
    phases = turn_count * (2.0 * math.pi / CHANNELS)
    cosine = jnp.cos(phases) / math.sqrt(CHANNELS)
    sine_part = jnp.sin(phases) / math.sqrt(CHANNELS)
    top_half = jnp.concatenate([cosine, -sine_part], axis=1)
    low_half = jnp.concatenate([sine_part, cosine], axis=1)
    return jnp.concatenate([top_half, low_half], axis=0).astype(jnp.bfloat16)


def compress(padded, range_code):
    gate_count = padded.shape[1] - 2 * CODE_REACH
    shape_out = (padded.shape[0], gate_count, padded.shape[3])
    real_sum = jnp.zeros(shape_out, jnp.float32)
    imag_sum = jnp.zeros(shape_out, jnp.float32)
    for offset in range(2 * CODE_REACH + 1):
        window = lax.slice_in_dim(padded, offset, offset + gate_count, axis=1).astype(jnp.float32)
        real_sum = (
            real_sum
            + range_code[0, offset] * window[:, :, 0]
            - range_code[1, offset] * window[:, :, 1]
        )
        imag_sum = (
            imag_sum
            + range_code[0, offset] * window[:, :, 1]
            + range_code[1, offset] * window[:, :, 0]
        )
    return jnp.stack([real_sum, imag_sum], axis=2).astype(jnp.bfloat16)


def local_gram(masked):
    real_rows = masked[:, :, 0]
    imag_rows = masked[:, :, 1]
    top_rows = jnp.concatenate([real_rows, imag_rows], axis=2)
    low_rows = jnp.concatenate([-imag_rows, real_rows], axis=2)
    stacked = jnp.concatenate([top_rows, low_rows], axis=1)
    return jnp.einsum("bri,brj->bij", stacked, stacked, preferred_element_type=jnp.float32)


def steering_table(steer_rows):
    element = jnp.arange(ELEMENTS, dtype=jnp.int32)
    turn_count = jnp.mod(
        element[None, :, None] * (2 * steer_rows[:, None, :] - ELEMENTS), 2 * ELEMENTS
    ).astype(jnp.float32)
    phases = turn_count * (math.pi / ELEMENTS)
    return jnp.concatenate([jnp.cos(phases), jnp.sin(phases)], axis=1)


def solve_all(factor, steering):
    return jax.vmap(
        lambda lower_part, target: jax.scipy.linalg.cho_solve((lower_part, True), target)
    )(factor, steering)


def beam_output(compressed, weights, steering):
    response = jnp.sum(steering * weights, axis=1)
    signal = compressed.astype(jnp.float32)
    weight_real = weights[:, :ELEMENTS]
    weight_imag = weights[:, ELEMENTS:]
    highest = lax.Precision.HIGHEST
    out_real = jnp.einsum(
        "bik,bgi->bkg", weight_real, signal[:, :, 0], precision=highest
    ) + jnp.einsum("bik,bgi->bkg", weight_imag, signal[:, :, 1], precision=highest)
    out_imag = jnp.einsum(
        "bik,bgi->bkg", weight_real, signal[:, :, 1], precision=highest
    ) - jnp.einsum("bik,bgi->bkg", weight_imag, signal[:, :, 0], precision=highest)
    return jnp.stack([out_real, out_imag], axis=0) / jnp.sqrt(response)[None, :, :, None]


def plain_shards(raw_samples, filter_taps, range_code, train_mask, steer_index):
    elem_dev = raw_samples.shape[0]
    gate_dev = raw_samples.shape[1]
    bin_dev = train_mask.shape[0]
    bin_total = bin_dev * lax.axis_size("dop")
    gates_total = gate_dev * lax.axis_size("rng")
    table = dft_table(bin_total)
    folded = raw_samples.astype(jnp.float32).reshape(elem_dev, gate_dev, 2, TAPS, CHANNELS)
    filtered = jnp.sum(folded * filter_taps, axis=3).astype(jnp.bfloat16)
    spectra = jnp.dot(
        filtered.reshape(elem_dev * gate_dev, 2 * CHANNELS),
        table,
        preferred_element_type=jnp.float32,
    )
    spectra = jnp.transpose(
        spectra.astype(jnp.bfloat16).reshape(elem_dev, gate_dev, 2, bin_total), (3, 1, 2, 0)
    )
    turned = lax.all_to_all(spectra, "dop", split_axis=0, concat_axis=3, tiled=True)
    padded = padded_2(turned, (("rng", 1),), CODE_REACH)
    compressed = compress(padded, range_code)
    masked = compressed * train_mask.astype(jnp.bfloat16)[:, :, None, None]
    dof_count = 2 * ELEMENTS
    identity = jnp.eye(dof_count, dtype=jnp.float32)
    steering = steering_table(steer_index)
    range_count = lax.axis_size("rng")
    owned_count = (bin_dev + range_count - 1) // range_count
    padded_bins = owned_count * range_count
    filled = jnp.pad(masked, ((0, padded_bins - bin_dev), (0, 0), (0, 0), (0, 0)))
    owned_rows = lax.all_to_all(filled, "rng", split_axis=0, concat_axis=1, tiled=True)
    owned_gram = local_gram(owned_rows) / gates_total + loading_level * identity
    owned_factor = jnp.linalg.cholesky(owned_gram)
    steer_filled = jnp.pad(steer_index, ((0, padded_bins - bin_dev), (0, 0)))
    first_bin = lax.axis_index("rng") * owned_count
    owned_steer = lax.dynamic_slice_in_dim(steer_filled, first_bin, owned_count, 0)
    owned_weights = solve_all(owned_factor, steering_table(owned_steer))
    weights = lax.all_gather(owned_weights, "rng", axis=0, tiled=True)[:bin_dev]
    return beam_output(compressed, weights, steering)


LANES = 128
MESH = pl.DeviceIdType.MESH
NT = (((1,), (1,)), ((), ()))


def pair_swapped(x, lane, slot):
    imag = jnp.mod(lane // slot, 2) == 1
    return jnp.where(imag, pltpu.roll(x, slot, 1), -pltpu.roll(x, LANES - slot, 1))


def greet(dops, rngs):
    d, r = lax.axis_index("dop"), lax.axis_index("rng")
    barrier = pltpu.get_barrier_semaphore()
    for i in range(1, dops):
        pl.semaphore_signal(
            barrier, inc=1, device_id=(lax.rem(d + i, dops), r), device_id_type=MESH
        )
    for j in range(1, rngs):
        pl.semaphore_signal(
            barrier, inc=1, device_id=(d, lax.rem(r + j, rngs)), device_id_type=MESH
        )


def exchange(dops, rngs, spec_ref, out_ref, send1, recv1, send2, recv2):
    d, r = lax.axis_index("dop"), lax.axis_index("rng")
    pl.semaphore_wait(pltpu.get_barrier_semaphore(), dops + rngs - 2)
    turns = []
    for i in range(1, dops):
        to = lax.rem(d + i, dops)
        turns.append(
            pltpu.make_async_remote_copy(
                src_ref=spec_ref.at[to],
                dst_ref=out_ref.at[r, d],
                send_sem=send1.at[i],
                recv_sem=recv1.at[i],
                device_id=(to, r),
                device_id_type=MESH,
            )
        )
        turns[-1].start()
    out_ref[r, d] = spec_ref[d]
    out_ref[r, dops] = spec_ref[dops]
    for copy in turns:
        copy.wait_recv()
    passed = []
    for j in range(1, rngs):
        copy = pltpu.make_async_remote_copy(
            src_ref=out_ref.at[r],
            dst_ref=out_ref.at[r],
            send_sem=send2.at[j],
            recv_sem=recv2.at[j],
            device_id=(d, lax.rem(r + j, rngs)),
            device_id_type=MESH,
        )
        copy.start()
        passed.append(copy)
    for copy in passed:
        copy.wait_recv()
    for copy in turns + passed:
        copy.wait_send()


def gather_kernel(
    raw_ref, taps_ref, table_ref, mask_ref, out_ref, filt_ref, spec_ref, own_ref, all_ref, *semaphores
):
    elems, gates = raw_ref.shape[0], raw_ref.shape[1]
    rngs, dops, rows = out_ref.shape[0], out_ref.shape[1] - 1, out_ref.shape[2]
    step, steps = pl.program_id(0), pl.num_programs(0)

    @pl.when(step == 0)
    def _():
        greet(dops, rngs)

    taps = []
    for t in range(TAPS):
        quarters = [
            jnp.broadcast_to(taps_ref[t : t + 1, i : i + LANES], (2, LANES))
            for i in range(0, CHANNELS, LANES)
        ]
        taps.append(jnp.concatenate(quarters, axis=0))
    for gate in range(gates):

        def one(e, carry, gate=gate):
            x = raw_ref[e, gate].astype(jnp.float32)
            terms = [x[8 * t : 8 * t + 8] * taps[t] for t in range(TAPS)]
            while len(terms) > 1:
                terms = [a + b for a, b in zip(terms[::2], terms[1::2])]
            at = pl.multiple_of((gate * elems + e) * 8, 8)
            filt_ref[pl.ds(at, 8), :] = terms[0]
            return carry

        lax.fori_loop(0, elems, one, 0, unroll=8)
    parts = [
        filt_ref[pl.ds(i, gates * elems, stride=8), :].astype(jnp.bfloat16) for i in range(8)
    ]
    chunk = lax.dot_general(
        table_ref[...], jnp.concatenate(parts, axis=1), NT, preferred_element_type=jnp.float32
    )
    lane = lax.broadcasted_iota(jnp.int32, (dops, LANES), 1)
    for q in range(gates):
        row = jnp.zeros((dops, LANES), jnp.float32)
        for c in range(LANES // elems):
            piece = chunk[c * dops : (c + 1) * dops]
            shift = ((c - q) * elems) % LANES
            if shift:
                piece = pltpu.roll(piece, shift, 1)
            row = jnp.where(lane // elems == c, piece, row)
        at = pl.multiple_of((step * gates + q) * dops, 8)
        spec_ref[pl.ds(at, dops), :] = row

    @pl.when(step == steps - 1)
    def _():
        full = steps * gates
        if rows > full:
            spec_ref[pl.ds(full * dops, (rows - full) * dops), :] = jnp.zeros(
                ((rows - full) * dops, LANES), jnp.float32
            )
        for d in range(dops):
            own_ref[d] = spec_ref[pl.ds(d, rows, stride=dops), :].astype(jnp.bfloat16)
        bins, own = mask_ref.shape
        held = mask_ref[...].astype(jnp.float32)
        lane = lax.broadcasted_iota(jnp.int32, (bins, LANES), 1)
        bin_row = lax.broadcasted_iota(jnp.int32, (bins, LANES), 0)
        spread = jnp.where(lane // (LANES // bins) == bin_row, 1.0, 0.0)
        column = lax.dot_general(
            held, spread, (((0,), (0,)), ((), ())), preferred_element_type=jnp.float32
        )
        column = jnp.concatenate([column, jnp.zeros((rows - own, LANES), jnp.float32)], axis=0)
        own_ref[dops] = column.astype(jnp.bfloat16)
        exchange(dops, rngs, own_ref, all_ref, *semaphores)
        out_ref[...] = all_ref[...]


def constant_table(bin_total):
    mode_index, bin_index = np.arange(CHANNELS), np.arange(bin_total)
    turn_count = np.mod(mode_index[:, None] * bin_index[None, :], CHANNELS).astype(np.float32)
    phases = turn_count * np.float32(2.0 * math.pi / CHANNELS)
    cosine = np.cos(phases) / np.float32(math.sqrt(CHANNELS))
    sine_part = np.sin(phases) / np.float32(math.sqrt(CHANNELS))
    table = np.block([[cosine, -sine_part], [sine_part, cosine]])
    return table.astype(ml_dtypes.bfloat16)


def gather(raw, filter_taps, train_mask, bin_total, dops, rngs, rows):
    elems, gates = raw.shape[0], raw.shape[1]
    bin_dev = bin_total // dops
    quarters = CHANNELS // LANES
    view = raw.reshape(elems, gates, 2, TAPS * quarters, LANES)
    view = jnp.transpose(view, (0, 1, 3, 2, 4)).reshape(elems, gates, 2 * TAPS * quarters, LANES)
    table = constant_table(bin_total).reshape(2, quarters, LANES, 2, dops, bin_dev)
    table = jnp.asarray(
        np.transpose(table, (5, 3, 4, 1, 0, 2)).reshape(2 * bin_total, 2 * CHANNELS)
    )
    block = LANES // elems
    return pl.pallas_call(
        gather_kernel,
        grid=(gates // block,),
        in_specs=[
            pl.BlockSpec((elems, block, 2 * TAPS * quarters, LANES), lambda i: (0, i, 0, 0)),
            pl.BlockSpec(filter_taps.shape, lambda i: (0, 0)),
            pl.BlockSpec(table.shape, lambda i: (0, 0)),
            pl.BlockSpec(train_mask.shape, lambda i: (0, 0)),
        ],
        out_specs=pl.BlockSpec(memory_space=pltpu.VMEM),
        out_shape=jax.ShapeDtypeStruct((rngs, dops + 1, rows, LANES), jnp.bfloat16),
        scratch_shapes=[
            pltpu.VMEM((elems * block * 8, LANES), jnp.float32),
            pltpu.VMEM((rows * dops, LANES), jnp.float32),
            pltpu.VMEM((dops + 1, rows, LANES), jnp.bfloat16),
            pltpu.VMEM((rngs, dops + 1, rows, LANES), jnp.bfloat16),
            pltpu.SemaphoreType.DMA((dops,)),
            pltpu.SemaphoreType.DMA((dops,)),
            pltpu.SemaphoreType.DMA((rngs,)),
            pltpu.SemaphoreType.DMA((rngs,)),
        ],
        compiler_params=pltpu.CompilerParams(
            collective_id=0, has_side_effects=True, vmem_limit_bytes=53 * 1024 * 1024
        ),
    )(view, filter_taps, table, train_mask)


def eliminate(a_re, a_im, b_re, b_im):
    size = a_re.shape[0]
    tiles = [[a_re[i : i + 8], a_im[i : i + 8]] for i in range(0, size, 8)] + [[b_re, b_im]]
    shape = (8, size)
    lane = lax.broadcasted_iota(jnp.int32, shape, 1)
    for p in range(0, size, 2):
        first, s = divmod(p, 8)

        def row(part, i):
            return jnp.broadcast_to(part[i : i + 1], shape)

        def column(part, i):
            return jnp.broadcast_to(part[:, i : i + 1], shape)

        u_re, u_im = (row(part, s) for part in tiles[first])
        v_re, v_im = (row(part, s + 1) for part in tiles[first])
        a, c = column(u_re, p), column(v_re, p + 1)
        b_re, b_im = column(u_re, p + 1), column(u_im, p + 1)
        inverse = 1.0 / (a * c - (b_re * b_re + b_im * b_im))
        one, two = lane == p, lane == p + 1
        pair = one | two
        u_re = jnp.where(pair, jnp.where(one, -1.0, 0.0), u_re)
        v_re = jnp.where(pair, jnp.where(two, -1.0, 0.0), v_re)
        u_im, v_im = jnp.where(pair, 0.0, u_im), jnp.where(pair, 0.0, v_im)
        f_re = (c * u_re - (b_re * v_re - b_im * v_im)) * inverse
        f_im = (c * u_im - (b_re * v_im + b_im * v_re)) * inverse
        g_re = (a * v_re - (b_re * u_re + b_im * u_im)) * inverse
        g_im = (a * v_im - (b_re * u_im - b_im * u_re)) * inverse
        begin = first + 1 if s == 6 else first
        for tile in tiles[begin:]:
            t_re, t_im = tile
            x_re, x_im = column(t_re, p), column(t_im, p)
            y_re, y_im = column(t_re, p + 1), column(t_im, p + 1)
            tile[0] = jnp.where(pair, 0.0, t_re) - (
                (x_re * f_re - x_im * f_im) + (y_re * g_re - y_im * g_im)
            )
            tile[1] = jnp.where(pair, 0.0, t_im) - (
                (x_re * f_im + x_im * f_re) + (y_re * g_im + y_im * g_re)
            )
    return tiles[-1]


def adapt_kernel(gate_dev, bin_dev, code_ref, steer_ref, rows_ref, out_ref, self_ref, turned_ref):
    rngs, dops = rows_ref.shape[0], rows_ref.shape[1] - 1
    gates = gate_dev * rngs
    slot = LANES // (2 * bin_dev)
    lane_dev = lax.broadcasted_iota(jnp.int32, (gate_dev, LANES), 1)
    lane = lax.broadcasted_iota(jnp.int32, (gates, LANES), 1)
    chosen = lax.rem(lax.axis_index("rng"), bin_dev)
    mask = jnp.concatenate(
        [rows_ref[r, dops].astype(jnp.float32)[:gate_dev] for r in range(rngs)], axis=0
    )
    signal, turned, train, train_turned = [], [], [], []
    edge = jnp.zeros((8, LANES), jnp.float32)
    for d in range(dops):
        for ref in (self_ref, turned_ref):
            ref[d, 0:8] = edge
            ref[d, 8 + gates : 16 + gates] = edge
        for r in range(rngs):
            y = rows_ref[r, d].astype(jnp.float32)[:gate_dev]
            at = 8 + r * gate_dev
            self_ref[d, at : at + gate_dev] = y
            turned_ref[d, at : at + gate_dev] = pair_swapped(y, lane_dev, slot)
        total = jnp.zeros((gates, LANES), jnp.float32)
        for t in range(2 * CODE_REACH + 1):
            at = 8 - CODE_REACH + t
            total = (
                total
                + code_ref[0:1, t : t + 1] * self_ref[d, at : at + gates]
                + code_ref[1:2, t : t + 1] * turned_ref[d, at : at + gates]
            )
        v = total.astype(jnp.bfloat16).astype(jnp.float32)
        q = pair_swapped(v, lane, slot)
        signal.append(v.astype(jnp.bfloat16))
        turned.append(q.astype(jnp.bfloat16))
        train.append((v * mask).astype(jnp.bfloat16))
        train_turned.append((q * mask).astype(jnp.bfloat16))

    def dot(a, b):
        return lax.dot_general(a, b, NT, preferred_element_type=jnp.float32)

    own = lane // (2 * slot) == chosen

    def of_bin(parts):
        kept = [jnp.where(own, x.astype(jnp.float32), 0.0).astype(jnp.bfloat16) for x in parts]
        return jnp.concatenate(kept, axis=1)

    signal_bins, train_bins = of_bin(signal), of_bin(train)
    signal, turned, train, train_turned = (
        jnp.concatenate(x, axis=1) for x in (signal, turned, train, train_turned)
    )
    all_re, all_im = dot(signal_bins, signal), dot(signal_bins, turned)
    gram_re, gram_im = dot(train_bins, train), dot(train_bins, train_turned)
    steer = steering_rows(steer_ref[...], chosen, dops, slot)
    high = steer.astype(jnp.bfloat16)
    rest = steer - high.astype(jnp.float32)
    middle = rest.astype(jnp.bfloat16)
    low = (rest - middle.astype(jnp.float32)).astype(jnp.bfloat16)
    looks = dot(high, signal) + (dot(middle, signal) + dot(low, signal))
    sights = dot(high, train) + (dot(middle, train) + dot(low, train))
    norms = jnp.sum(steer * steer, axis=1, keepdims=True)
    beams = steer.shape[0] // 2
    diagonal = (
        lax.broadcasted_iota(jnp.int32, (gates, gates), 0)
        == lax.broadcasted_iota(jnp.int32, (gates, gates), 1)
    )
    loading = jnp.where(diagonal, loading_level * gates, 0.0)
    b_re, b_im = sights[:beams], sights[beams:]
    spare = jnp.zeros((8 - beams, gates), jnp.float32)
    sides = [jnp.concatenate([x, spare], axis=0) for x in (b_re, b_im)]
    y_re, y_im = (x[:beams] for x in eliminate(gram_re + loading, -gram_im, *sides))
    highest = lax.Precision.HIGHEST
    both = jnp.concatenate([y_re, y_im], axis=0)
    by_re = jnp.dot(both, all_re, precision=highest, preferred_element_type=jnp.float32)
    by_im = jnp.dot(both, all_im, precision=highest, preferred_element_type=jnp.float32)
    o_re = looks[:beams] - (by_re[:beams] + by_im[beams:])
    o_im = looks[beams:] - (by_re[beams:] - by_im[:beams])
    lost = jnp.sum(b_re * y_re + b_im * y_im, axis=1, keepdims=True)
    response = (norms[:beams] - lost) / loading_level
    scale = 1.0 / (loading_level * jnp.sqrt(response))
    out = jnp.concatenate([o_re * scale, o_im * scale], axis=0)
    if gates < LANES:
        out = jnp.concatenate(
            [out, jnp.zeros((2 * beams, LANES - gates), jnp.float32)], axis=1
        )
    out_ref[...] = out


def swap_kernel(gate_dev, rngs, mine_ref, out_ref, other_ref, send, recv):
    d, r = lax.axis_index("dop"), lax.axis_index("rng")
    chosen = lax.rem(r, 2)
    partner = (d, r + 1 - 2 * chosen)
    barrier = pltpu.get_barrier_semaphore()
    pl.semaphore_signal(barrier, inc=1, device_id=partner, device_id_type=MESH)
    pl.semaphore_wait(barrier, 1)
    copy = pltpu.make_async_remote_copy(
        src_ref=mine_ref,
        dst_ref=other_ref,
        send_sem=send,
        recv_sem=recv,
        device_id=partner,
        device_id_type=MESH,
    )
    copy.start()
    copy.wait()
    beams = mine_ref.shape[0] // 2

    def own_gates(x):
        out = x[:, :gate_dev]
        for i in range(1, rngs):
            out = jnp.where(r == i, x[:, i * gate_dev : (i + 1) * gate_dev], out)
        return out

    mine, other = own_gates(mine_ref[...]), own_gates(other_ref[...])
    for k in range(2):
        both = jnp.where(chosen == k, mine, other)
        for part in range(2):
            out_ref[part, k] = both[part * beams : (part + 1) * beams]


def swap(mine, gate_dev, rngs):
    vmem = pl.BlockSpec(memory_space=pltpu.VMEM)
    return pl.pallas_call(
        lambda *refs: swap_kernel(gate_dev, rngs, *refs),
        in_specs=[vmem],
        out_specs=vmem,
        out_shape=jax.ShapeDtypeStruct((2, 2, mine.shape[0] // 2, gate_dev), jnp.float32),
        scratch_shapes=[
            pltpu.VMEM(mine.shape, jnp.float32),
            pltpu.SemaphoreType.DMA,
            pltpu.SemaphoreType.DMA,
        ],
        compiler_params=pltpu.CompilerParams(
            collective_id=1, has_side_effects=True, vmem_limit_bytes=8 * 1024 * 1024
        ),
    )(mine)


def cosine_of_turn(turn):
    right = ELEMENTS // 2
    quadrant = (turn + right // 2) // right
    x = (turn - quadrant * right).astype(jnp.float32) * (math.pi / ELEMENTS)
    z = x * x
    sine_part = x + x * z * (-1.6666654611e-1 + z * (8.3321608736e-3 - z * 1.9515295891e-4))
    cosine = 1.0 - 0.5 * z + z * z * (
        4.166664568298827e-2 + z * (-1.388731625493765e-3 + z * 2.443315711809948e-5)
    )
    odd = jnp.bitwise_and(quadrant, 1) == 1
    value = jnp.where(odd, sine_part, cosine)
    flip = (quadrant == 1) | (quadrant == 2)
    return jnp.where(flip, -value, value)


def steering_rows(steer_index, chosen, dops, slot):
    bins, beams = steer_index.shape
    picked = steer_index[:1]
    for k in range(1, bins):
        picked = jnp.where(chosen == k, steer_index[k : k + 1], picked)
    looks = [jnp.broadcast_to(picked[:, j : j + 1], (1, LANES)) for j in range(beams)]
    look = 2 * jnp.concatenate(looks + looks, axis=0) - ELEMENTS
    lane = lax.broadcasted_iota(jnp.int32, look.shape, 1)
    row = lax.broadcasted_iota(jnp.int32, look.shape, 0)
    own = lane // (2 * slot) == chosen
    quarter = (ELEMENTS // 2) * (row // beams - (lane // slot) % 2)
    parts = []
    for d in range(dops):
        element = d * slot + lane % slot
        turn = jnp.bitwise_and(element * look + quarter, 2 * ELEMENTS - 1)
        parts.append(jnp.where(own, cosine_of_turn(turn), 0.0))
    return jnp.concatenate(parts, axis=1)


def adapt(rows, range_code, steer, gate_dev, bin_dev):
    rngs, dops = rows.shape[0], rows.shape[1] - 1
    gates = gate_dev * rngs
    beams = steer.shape[1]
    vmem = pl.BlockSpec(memory_space=pltpu.VMEM)
    return pl.pallas_call(
        lambda *refs: adapt_kernel(gate_dev, bin_dev, *refs),
        in_specs=[vmem, vmem, vmem],
        out_specs=vmem,
        out_shape=jax.ShapeDtypeStruct((2 * beams, LANES), jnp.float32),
        scratch_shapes=[pltpu.VMEM((dops, gates + 16, LANES), jnp.float32)] * 2,
        compiler_params=pltpu.CompilerParams(vmem_limit_bytes=32 * 1024 * 1024),
    )(range_code, steer, rows)


def dual_shards(raw_samples, filter_taps, range_code, train_mask, steer_index):
    elem_dev, gate_dev = raw_samples.shape[:2]
    bin_dev = train_mask.shape[0]
    dops, rngs = lax.axis_size("dop"), lax.axis_size("rng")
    rows = -(-gate_dev // 16) * 16
    total = bin_dev * dops
    gathered = gather(raw_samples, filter_taps, train_mask, total, dops, rngs, rows)
    mine = adapt(gathered, range_code, steer_index, gate_dev, bin_dev)
    return swap(mine, gate_dev, rngs)


def shards(raw_samples, filter_taps, range_code, train_mask, steer_index):
    elem_dev, gate_dev = raw_samples.shape[:2]
    dops, rngs = lax.axis_size("dop"), lax.axis_size("rng")
    fits = (
        2 * train_mask.shape[0] * elem_dev == LANES
        and dops == 8
        and train_mask.shape[0] == 2
        and rngs % 2 == 0
        and steer_index.shape[1] <= 8
        and gate_dev % 8 == 0
        and gate_dev * rngs <= LANES
    )
    path = dual_shards if fits else plain_shards
    return path(raw_samples, filter_taps, range_code, train_mask, steer_index)


def solution(mesh):
    return jax.shard_map(
        shards,
        mesh=mesh,
        in_specs=(P("dop", "rng", None, None), P(), P(), P("dop", "rng"), P("dop", None)),
        out_specs=P(None, "dop", None, "rng"),
        check_vma=False,
    )
```

```python
import math

import jax
import jax.numpy as jnp
import ml_dtypes
import numpy as np
from jax import lax
from jax.experimental import pallas as pl
from jax.experimental.pallas import tpu as pltpu
from jax.sharding import PartitionSpec as P

ELEMENTS = 256
CHANNELS = 512
TAPS = 8
CODE_REACH = 3


loading_level = 0.25


def padded_2(x, sides, width):
    for axis, dim in sides:
        count, length = (lax.axis_size(axis), x.shape[dim])
        up = [(i, (i + 1) % count) for i in range(count - 1)]
        down = [(j, i) for i, j in up]
        last = lax.slice_in_dim(x, length - width, length, axis=dim)
        leading = lax.slice_in_dim(x, 0, width, axis=dim)
        before = lax.ppermute(last, axis, up)
        after = lax.ppermute(leading, axis, down)
        x = jnp.concatenate([before, x, after], axis=dim)
    return x


def dft_table(bin_total):
    mode_index = jnp.arange(CHANNELS, dtype=jnp.int32)
    bin_index = jnp.arange(bin_total, dtype=jnp.int32)
    turn_count = jnp.mod(mode_index[:, None] * bin_index[None, :], CHANNELS).astype(jnp.float32)
    phases = turn_count * (2.0 * math.pi / CHANNELS)
    cosine = jnp.cos(phases) / math.sqrt(CHANNELS)
    sine_part = jnp.sin(phases) / math.sqrt(CHANNELS)
    top_half = jnp.concatenate([cosine, -sine_part], axis=1)
    low_half = jnp.concatenate([sine_part, cosine], axis=1)
    return jnp.concatenate([top_half, low_half], axis=0).astype(jnp.bfloat16)


def compress(padded, range_code):
    gate_count = padded.shape[1] - 2 * CODE_REACH
    shape_out = (padded.shape[0], gate_count, padded.shape[3])
    real_sum = jnp.zeros(shape_out, jnp.float32)
    imag_sum = jnp.zeros(shape_out, jnp.float32)
    for offset in range(2 * CODE_REACH + 1):
        window = lax.slice_in_dim(padded, offset, offset + gate_count, axis=1).astype(jnp.float32)
        real_sum = (
            real_sum
            + range_code[0, offset] * window[:, :, 0]
            - range_code[1, offset] * window[:, :, 1]
        )
        imag_sum = (
            imag_sum
            + range_code[0, offset] * window[:, :, 1]
            + range_code[1, offset] * window[:, :, 0]
        )
    return jnp.stack([real_sum, imag_sum], axis=2).astype(jnp.bfloat16)


def local_gram(masked):
    real_rows = masked[:, :, 0]
    imag_rows = masked[:, :, 1]
    top_rows = jnp.concatenate([real_rows, imag_rows], axis=2)
    low_rows = jnp.concatenate([-imag_rows, real_rows], axis=2)
    stacked = jnp.concatenate([top_rows, low_rows], axis=1)
    return jnp.einsum("bri,brj->bij", stacked, stacked, preferred_element_type=jnp.float32)


def steering_table(steer_rows):
    element = jnp.arange(ELEMENTS, dtype=jnp.int32)
    turn_count = jnp.mod(
        element[None, :, None] * (2 * steer_rows[:, None, :] - ELEMENTS), 2 * ELEMENTS
    ).astype(jnp.float32)
    phases = turn_count * (math.pi / ELEMENTS)
    return jnp.concatenate([jnp.cos(phases), jnp.sin(phases)], axis=1)


def solve_all(factor, steering):
    return jax.vmap(
        lambda lower_part, target: jax.scipy.linalg.cho_solve((lower_part, True), target)
    )(factor, steering)


def beam_output(compressed, weights, steering):
    response = jnp.sum(steering * weights, axis=1)
    signal = compressed.astype(jnp.float32)
    weight_real = weights[:, :ELEMENTS]
    weight_imag = weights[:, ELEMENTS:]
    highest = lax.Precision.HIGHEST
    out_real = jnp.einsum(
        "bik,bgi->bkg", weight_real, signal[:, :, 0], precision=highest
    ) + jnp.einsum("bik,bgi->bkg", weight_imag, signal[:, :, 1], precision=highest)
    out_imag = jnp.einsum(
        "bik,bgi->bkg", weight_real, signal[:, :, 1], precision=highest
    ) - jnp.einsum("bik,bgi->bkg", weight_imag, signal[:, :, 0], precision=highest)
    return jnp.stack([out_real, out_imag], axis=0) / jnp.sqrt(response)[None, :, :, None]


def plain_shards(raw_samples, filter_taps, range_code, train_mask, steer_index):
    elem_dev = raw_samples.shape[0]
    gate_dev = raw_samples.shape[1]
    bin_dev = train_mask.shape[0]
    bin_total = bin_dev * lax.axis_size("dop")
    gates_total = gate_dev * lax.axis_size("rng")
    table = dft_table(bin_total)
    folded = raw_samples.astype(jnp.float32).reshape(elem_dev, gate_dev, 2, TAPS, CHANNELS)
    filtered = jnp.sum(folded * filter_taps, axis=3).astype(jnp.bfloat16)
    spectra = jnp.dot(
        filtered.reshape(elem_dev * gate_dev, 2 * CHANNELS),
        table,
        preferred_element_type=jnp.float32,
    )
    spectra = jnp.transpose(
        spectra.astype(jnp.bfloat16).reshape(elem_dev, gate_dev, 2, bin_total), (3, 1, 2, 0)
    )
    turned = lax.all_to_all(spectra, "dop", split_axis=0, concat_axis=3, tiled=True)
    padded = padded_2(turned, (("rng", 1),), CODE_REACH)
    compressed = compress(padded, range_code)
    masked = compressed * train_mask.astype(jnp.bfloat16)[:, :, None, None]
    dof_count = 2 * ELEMENTS
    identity = jnp.eye(dof_count, dtype=jnp.float32)
    steering = steering_table(steer_index)
    range_count = lax.axis_size("rng")
    owned_count = (bin_dev + range_count - 1) // range_count
    padded_bins = owned_count * range_count
    filled = jnp.pad(masked, ((0, padded_bins - bin_dev), (0, 0), (0, 0), (0, 0)))
    owned_rows = lax.all_to_all(filled, "rng", split_axis=0, concat_axis=1, tiled=True)
    owned_gram = local_gram(owned_rows) / gates_total + loading_level * identity
    owned_factor = jnp.linalg.cholesky(owned_gram)
    steer_filled = jnp.pad(steer_index, ((0, padded_bins - bin_dev), (0, 0)))
    first_bin = lax.axis_index("rng") * owned_count
    owned_steer = lax.dynamic_slice_in_dim(steer_filled, first_bin, owned_count, 0)
    owned_weights = solve_all(owned_factor, steering_table(owned_steer))
    weights = lax.all_gather(owned_weights, "rng", axis=0, tiled=True)[:bin_dev]
    return beam_output(compressed, weights, steering)


LANES = 128
MESH = pl.DeviceIdType.MESH
NT = (((1,), (1,)), ((), ()))


def pair_swapped(x, lane, slot):
    imag = jnp.mod(lane // slot, 2) == 1
    return jnp.where(imag, pltpu.roll(x, slot, 1), -pltpu.roll(x, LANES - slot, 1))


def greet(dops, rngs):
    d, r = lax.axis_index("dop"), lax.axis_index("rng")
    barrier = pltpu.get_barrier_semaphore()
    for i in range(1, dops):
        pl.semaphore_signal(
            barrier, inc=1, device_id=(lax.rem(d + i, dops), r), device_id_type=MESH
        )
    for j in range(1, rngs):
        pl.semaphore_signal(
            barrier, inc=1, device_id=(d, lax.rem(r + j, rngs)), device_id_type=MESH
        )


def exchange(dops, rngs, spec_ref, out_ref, send1, recv1, send2, recv2):
    d, r = lax.axis_index("dop"), lax.axis_index("rng")
    pl.semaphore_wait(pltpu.get_barrier_semaphore(), dops + rngs - 2)
    turns = []
    for i in range(1, dops):
        to = lax.rem(d + i, dops)
        turns.append(
            pltpu.make_async_remote_copy(
                src_ref=spec_ref.at[to],
                dst_ref=out_ref.at[r, d],
                send_sem=send1.at[i],
                recv_sem=recv1.at[i],
                device_id=(to, r),
                device_id_type=MESH,
            )
        )
        turns[-1].start()
    out_ref[r, d] = spec_ref[d]
    out_ref[r, dops] = spec_ref[dops]
    for copy in turns:
        copy.wait_recv()
    passed = []
    for j in range(1, rngs):
        copy = pltpu.make_async_remote_copy(
            src_ref=out_ref.at[r],
            dst_ref=out_ref.at[r],
            send_sem=send2.at[j],
            recv_sem=recv2.at[j],
            device_id=(d, lax.rem(r + j, rngs)),
            device_id_type=MESH,
        )
        copy.start()
        passed.append(copy)
    for copy in passed:
        copy.wait_recv()
    for copy in turns + passed:
        copy.wait_send()


def gather_kernel(
    raw_ref, taps_ref, table_ref, mask_ref, out_ref, filt_ref, spec_ref, own_ref, all_ref, *semaphores
):
    elems, gates = raw_ref.shape[0], raw_ref.shape[1]
    rngs, dops, rows = out_ref.shape[0], out_ref.shape[1] - 1, out_ref.shape[2]
    step, steps = pl.program_id(0), pl.num_programs(0)

    @pl.when(step == 0)
    def _():
        greet(dops, rngs)

    taps = []
    for t in range(TAPS):
        quarters = [
            jnp.broadcast_to(taps_ref[t : t + 1, i : i + LANES], (2, LANES))
            for i in range(0, CHANNELS, LANES)
        ]
        taps.append(jnp.concatenate(quarters, axis=0))
    for gate in range(gates):

        def one(e, carry, gate=gate):
            x = raw_ref[e, gate].astype(jnp.float32)
            terms = [x[8 * t : 8 * t + 8] * taps[t] for t in range(TAPS)]
            while len(terms) > 1:
                terms = [a + b for a, b in zip(terms[::2], terms[1::2])]
            at = pl.multiple_of((gate * elems + e) * 8, 8)
            filt_ref[pl.ds(at, 8), :] = terms[0]
            return carry

        lax.fori_loop(0, elems, one, 0, unroll=8)
    parts = [
        filt_ref[pl.ds(i, gates * elems, stride=8), :].astype(jnp.bfloat16) for i in range(8)
    ]
    chunk = lax.dot_general(
        table_ref[...], jnp.concatenate(parts, axis=1), NT, preferred_element_type=jnp.float32
    )
    lane = lax.broadcasted_iota(jnp.int32, (dops, LANES), 1)
    for q in range(gates):
        row = jnp.zeros((dops, LANES), jnp.float32)
        for c in range(LANES // elems):
            piece = chunk[c * dops : (c + 1) * dops]
            shift = ((c - q) * elems) % LANES
            if shift:
                piece = pltpu.roll(piece, shift, 1)
            row = jnp.where(lane // elems == c, piece, row)
        at = pl.multiple_of((step * gates + q) * dops, 8)
        spec_ref[pl.ds(at, dops), :] = row

    @pl.when(step == steps - 1)
    def _():
        full = steps * gates
        if rows > full:
            spec_ref[pl.ds(full * dops, (rows - full) * dops), :] = jnp.zeros(
                ((rows - full) * dops, LANES), jnp.float32
            )
        for d in range(dops):
            own_ref[d] = spec_ref[pl.ds(d, rows, stride=dops), :].astype(jnp.bfloat16)
        bins, own = mask_ref.shape
        held = mask_ref[...].astype(jnp.float32)
        lane = lax.broadcasted_iota(jnp.int32, (bins, LANES), 1)
        bin_row = lax.broadcasted_iota(jnp.int32, (bins, LANES), 0)
        spread = jnp.where(lane // (LANES // bins) == bin_row, 1.0, 0.0)
        column = lax.dot_general(
            held, spread, (((0,), (0,)), ((), ())), preferred_element_type=jnp.float32
        )
        column = jnp.concatenate([column, jnp.zeros((rows - own, LANES), jnp.float32)], axis=0)
        own_ref[dops] = column.astype(jnp.bfloat16)
        exchange(dops, rngs, own_ref, all_ref, *semaphores)
        out_ref[...] = all_ref[...]


def constant_table(bin_total):
    mode_index, bin_index = np.arange(CHANNELS), np.arange(bin_total)
    turn_count = np.mod(mode_index[:, None] * bin_index[None, :], CHANNELS).astype(np.float32)
    phases = turn_count * np.float32(2.0 * math.pi / CHANNELS)
    cosine = np.cos(phases) / np.float32(math.sqrt(CHANNELS))
    sine_part = np.sin(phases) / np.float32(math.sqrt(CHANNELS))
    table = np.block([[cosine, -sine_part], [sine_part, cosine]])
    return table.astype(ml_dtypes.bfloat16)


def gather(raw, filter_taps, train_mask, bin_total, dops, rngs, rows):
    elems, gates = raw.shape[0], raw.shape[1]
    bin_dev = bin_total // dops
    quarters = CHANNELS // LANES
    view = raw.reshape(elems, gates, 2, TAPS * quarters, LANES)
    view = jnp.transpose(view, (0, 1, 3, 2, 4)).reshape(elems, gates, 2 * TAPS * quarters, LANES)
    table = constant_table(bin_total).reshape(2, quarters, LANES, 2, dops, bin_dev)
    table = jnp.asarray(
        np.transpose(table, (5, 3, 4, 1, 0, 2)).reshape(2 * bin_total, 2 * CHANNELS)
    )
    block = LANES // elems
    return pl.pallas_call(
        gather_kernel,
        grid=(gates // block,),
        in_specs=[
            pl.BlockSpec((elems, block, 2 * TAPS * quarters, LANES), lambda i: (0, i, 0, 0)),
            pl.BlockSpec(filter_taps.shape, lambda i: (0, 0)),
            pl.BlockSpec(table.shape, lambda i: (0, 0)),
            pl.BlockSpec(train_mask.shape, lambda i: (0, 0)),
        ],
        out_specs=pl.BlockSpec(memory_space=pltpu.VMEM),
        out_shape=jax.ShapeDtypeStruct((rngs, dops + 1, rows, LANES), jnp.bfloat16),
        scratch_shapes=[
            pltpu.VMEM((elems * block * 8, LANES), jnp.float32),
            pltpu.VMEM((rows * dops, LANES), jnp.float32),
            pltpu.VMEM((dops + 1, rows, LANES), jnp.bfloat16),
            pltpu.VMEM((rngs, dops + 1, rows, LANES), jnp.bfloat16),
            pltpu.SemaphoreType.DMA((dops,)),
            pltpu.SemaphoreType.DMA((dops,)),
            pltpu.SemaphoreType.DMA((rngs,)),
            pltpu.SemaphoreType.DMA((rngs,)),
        ],
        compiler_params=pltpu.CompilerParams(
            collective_id=0, has_side_effects=True, vmem_limit_bytes=56 * 1024 * 1024
        ),
    )(view, filter_taps, table, train_mask)


def eliminate(a_re, a_im, b_re, b_im):
    size = a_re.shape[0]
    tiles = [[a_re[i : i + 8], a_im[i : i + 8]] for i in range(0, size, 8)] + [[b_re, b_im]]
    shape = (8, size)
    lane = lax.broadcasted_iota(jnp.int32, shape, 1)
    for p in range(0, size, 2):
        first, s = divmod(p, 8)

        def row(part, i):
            return jnp.broadcast_to(part[i : i + 1], shape)

        def column(part, i):
            return jnp.broadcast_to(part[:, i : i + 1], shape)

        u_re, u_im = (row(part, s) for part in tiles[first])
        v_re, v_im = (row(part, s + 1) for part in tiles[first])
        a, c = column(u_re, p), column(v_re, p + 1)
        b_re, b_im = column(u_re, p + 1), column(u_im, p + 1)
        inverse = 1.0 / (a * c - (b_re * b_re + b_im * b_im))
        one, two = lane == p, lane == p + 1
        pair = one | two
        u_re = jnp.where(pair, jnp.where(one, -1.0, 0.0), u_re)
        v_re = jnp.where(pair, jnp.where(two, -1.0, 0.0), v_re)
        u_im, v_im = jnp.where(pair, 0.0, u_im), jnp.where(pair, 0.0, v_im)
        f_re = (c * u_re - (b_re * v_re - b_im * v_im)) * inverse
        f_im = (c * u_im - (b_re * v_im + b_im * v_re)) * inverse
        g_re = (a * v_re - (b_re * u_re + b_im * u_im)) * inverse
        g_im = (a * v_im - (b_re * u_im - b_im * u_re)) * inverse
        begin = first + 1 if s == 6 else first
        for tile in tiles[begin:]:
            t_re, t_im = tile
            x_re, x_im = column(t_re, p), column(t_im, p)
            y_re, y_im = column(t_re, p + 1), column(t_im, p + 1)
            tile[0] = jnp.where(pair, 0.0, t_re) - (
                (x_re * f_re - x_im * f_im) + (y_re * g_re - y_im * g_im)
            )
            tile[1] = jnp.where(pair, 0.0, t_im) - (
                (x_re * f_im + x_im * f_re) + (y_re * g_im + y_im * g_re)
            )
    return tiles[-1]


def adapt_kernel(gate_dev, bin_dev, code_ref, steer_ref, rows_ref, out_ref, self_ref, turned_ref):
    rngs, dops = rows_ref.shape[0], rows_ref.shape[1] - 1
    gates = gate_dev * rngs
    slot = LANES // (2 * bin_dev)
    lane_dev = lax.broadcasted_iota(jnp.int32, (gate_dev, LANES), 1)
    lane = lax.broadcasted_iota(jnp.int32, (gates, LANES), 1)
    chosen = lax.rem(lax.axis_index("rng"), bin_dev)
    mask = jnp.concatenate(
        [rows_ref[r, dops].astype(jnp.float32)[:gate_dev] for r in range(rngs)], axis=0
    )
    signal, turned, train, train_turned = [], [], [], []
    edge = jnp.zeros((8, LANES), jnp.float32)
    for d in range(dops):
        for ref in (self_ref, turned_ref):
            ref[d, 0:8] = edge
            ref[d, 8 + gates : 16 + gates] = edge
        for r in range(rngs):
            y = rows_ref[r, d].astype(jnp.float32)[:gate_dev]
            at = 8 + r * gate_dev
            self_ref[d, at : at + gate_dev] = y
            turned_ref[d, at : at + gate_dev] = pair_swapped(y, lane_dev, slot)
        total = jnp.zeros((gates, LANES), jnp.float32)
        for t in range(2 * CODE_REACH + 1):
            at = 8 - CODE_REACH + t
            total = (
                total
                + code_ref[0:1, t : t + 1] * self_ref[d, at : at + gates]
                + code_ref[1:2, t : t + 1] * turned_ref[d, at : at + gates]
            )
        v = total.astype(jnp.bfloat16).astype(jnp.float32)
        q = pair_swapped(v, lane, slot)
        signal.append(v.astype(jnp.bfloat16))
        turned.append(q.astype(jnp.bfloat16))
        train.append((v * mask).astype(jnp.bfloat16))
        train_turned.append((q * mask).astype(jnp.bfloat16))

    def dot(a, b):
        return lax.dot_general(a, b, NT, preferred_element_type=jnp.float32)

    own = lane // (2 * slot) == chosen

    def of_bin(parts):
        kept = [jnp.where(own, x.astype(jnp.float32), 0.0).astype(jnp.bfloat16) for x in parts]
        return jnp.concatenate(kept, axis=1)

    signal_bins, train_bins = of_bin(signal), of_bin(train)
    signal, turned, train, train_turned = (
        jnp.concatenate(x, axis=1) for x in (signal, turned, train, train_turned)
    )
    all_re, all_im = dot(signal_bins, signal), dot(signal_bins, turned)
    gram_re, gram_im = dot(train_bins, train), dot(train_bins, train_turned)
    steer = steering_rows(steer_ref[...], chosen, dops, slot)
    high = steer.astype(jnp.bfloat16)
    rest = steer - high.astype(jnp.float32)
    middle = rest.astype(jnp.bfloat16)
    low = (rest - middle.astype(jnp.float32)).astype(jnp.bfloat16)
    looks = dot(high, signal) + (dot(middle, signal) + dot(low, signal))
    sights = dot(high, train) + (dot(middle, train) + dot(low, train))
    norms = jnp.sum(steer * steer, axis=1, keepdims=True)
    beams = steer.shape[0] // 2
    diagonal = (
        lax.broadcasted_iota(jnp.int32, (gates, gates), 0)
        == lax.broadcasted_iota(jnp.int32, (gates, gates), 1)
    )
    loading = jnp.where(diagonal, loading_level * gates, 0.0)
    b_re, b_im = sights[:beams], sights[beams:]
    spare = jnp.zeros((8 - beams, gates), jnp.float32)
    sides = [jnp.concatenate([x, spare], axis=0) for x in (b_re, b_im)]
    y_re, y_im = (x[:beams] for x in eliminate(gram_re + loading, -gram_im, *sides))
    highest = lax.Precision.HIGHEST
    both = jnp.concatenate([y_re, y_im], axis=0)
    by_re = jnp.dot(both, all_re, precision=highest, preferred_element_type=jnp.float32)
    by_im = jnp.dot(both, all_im, precision=highest, preferred_element_type=jnp.float32)
    o_re = looks[:beams] - (by_re[:beams] + by_im[beams:])
    o_im = looks[beams:] - (by_re[beams:] - by_im[:beams])
    lost = jnp.sum(b_re * y_re + b_im * y_im, axis=1, keepdims=True)
    response = (norms[:beams] - lost) / loading_level
    scale = 1.0 / (loading_level * jnp.sqrt(response))
    out = jnp.concatenate([o_re * scale, o_im * scale], axis=0)
    if gates < LANES:
        out = jnp.concatenate(
            [out, jnp.zeros((2 * beams, LANES - gates), jnp.float32)], axis=1
        )
    out_ref[...] = out


def swap_kernel(gate_dev, rngs, mine_ref, out_ref, other_ref, send, recv):
    d, r = lax.axis_index("dop"), lax.axis_index("rng")
    chosen = lax.rem(r, 2)
    partner = (d, r + 1 - 2 * chosen)
    barrier = pltpu.get_barrier_semaphore()
    pl.semaphore_signal(barrier, inc=1, device_id=partner, device_id_type=MESH)
    pl.semaphore_wait(barrier, 1)
    copy = pltpu.make_async_remote_copy(
        src_ref=mine_ref,
        dst_ref=other_ref,
        send_sem=send,
        recv_sem=recv,
        device_id=partner,
        device_id_type=MESH,
    )
    copy.start()
    copy.wait()
    beams = mine_ref.shape[0] // 2

    def own_gates(x):
        out = x[:, :gate_dev]
        for i in range(1, rngs):
            out = jnp.where(r == i, x[:, i * gate_dev : (i + 1) * gate_dev], out)
        return out

    mine, other = own_gates(mine_ref[...]), own_gates(other_ref[...])
    for k in range(2):
        both = jnp.where(chosen == k, mine, other)
        for part in range(2):
            out_ref[part, k] = both[part * beams : (part + 1) * beams]


def swap(mine, gate_dev, rngs):
    vmem = pl.BlockSpec(memory_space=pltpu.VMEM)
    return pl.pallas_call(
        lambda *refs: swap_kernel(gate_dev, rngs, *refs),
        in_specs=[vmem],
        out_specs=vmem,
        out_shape=jax.ShapeDtypeStruct((2, 2, mine.shape[0] // 2, gate_dev), jnp.float32),
        scratch_shapes=[
            pltpu.VMEM(mine.shape, jnp.float32),
            pltpu.SemaphoreType.DMA,
            pltpu.SemaphoreType.DMA,
        ],
        compiler_params=pltpu.CompilerParams(
            collective_id=1, has_side_effects=True, vmem_limit_bytes=56 * 1024 * 1024
        ),
    )(mine)


def cosine_of_turn(turn):
    right = ELEMENTS // 2
    quadrant = (turn + right // 2) // right
    x = (turn - quadrant * right).astype(jnp.float32) * (math.pi / ELEMENTS)
    z = x * x
    sine_part = x + x * z * (-1.6666654611e-1 + z * (8.3321608736e-3 - z * 1.9515295891e-4))
    cosine = 1.0 - 0.5 * z + z * z * (
        4.166664568298827e-2 + z * (-1.388731625493765e-3 + z * 2.443315711809948e-5)
    )
    odd = jnp.bitwise_and(quadrant, 1) == 1
    value = jnp.where(odd, sine_part, cosine)
    flip = (quadrant == 1) | (quadrant == 2)
    return jnp.where(flip, -value, value)


def steering_rows(steer_index, chosen, dops, slot):
    bins, beams = steer_index.shape
    picked = steer_index[:1]
    for k in range(1, bins):
        picked = jnp.where(chosen == k, steer_index[k : k + 1], picked)
    looks = [jnp.broadcast_to(picked[:, j : j + 1], (1, LANES)) for j in range(beams)]
    look = 2 * jnp.concatenate(looks + looks, axis=0) - ELEMENTS
    lane = lax.broadcasted_iota(jnp.int32, look.shape, 1)
    row = lax.broadcasted_iota(jnp.int32, look.shape, 0)
    own = lane // (2 * slot) == chosen
    quarter = (ELEMENTS // 2) * (row // beams - (lane // slot) % 2)
    parts = []
    for d in range(dops):
        element = d * slot + lane % slot
        turn = jnp.bitwise_and(element * look + quarter, 2 * ELEMENTS - 1)
        parts.append(jnp.where(own, cosine_of_turn(turn), 0.0))
    return jnp.concatenate(parts, axis=1)


def adapt(rows, range_code, steer, gate_dev, bin_dev):
    rngs, dops = rows.shape[0], rows.shape[1] - 1
    gates = gate_dev * rngs
    beams = steer.shape[1]
    vmem = pl.BlockSpec(memory_space=pltpu.VMEM)
    return pl.pallas_call(
        lambda *refs: adapt_kernel(gate_dev, bin_dev, *refs),
        in_specs=[vmem, vmem, vmem],
        out_specs=vmem,
        out_shape=jax.ShapeDtypeStruct((2 * beams, LANES), jnp.float32),
        scratch_shapes=[pltpu.VMEM((dops, gates + 16, LANES), jnp.float32)] * 2,
        compiler_params=pltpu.CompilerParams(vmem_limit_bytes=56 * 1024 * 1024),
    )(range_code, steer, rows)


def dual_shards(raw_samples, filter_taps, range_code, train_mask, steer_index):
    elem_dev, gate_dev = raw_samples.shape[:2]
    bin_dev = train_mask.shape[0]
    dops, rngs = lax.axis_size("dop"), lax.axis_size("rng")
    rows = -(-gate_dev // 16) * 16
    total = bin_dev * dops
    gathered = gather(raw_samples, filter_taps, train_mask, total, dops, rngs, rows)
    mine = adapt(gathered, range_code, steer_index, gate_dev, bin_dev)
    return swap(mine, gate_dev, rngs)


def shards(raw_samples, filter_taps, range_code, train_mask, steer_index):
    elem_dev, gate_dev = raw_samples.shape[:2]
    dops, rngs = lax.axis_size("dop"), lax.axis_size("rng")
    fits = (
        2 * train_mask.shape[0] * elem_dev == LANES
        and dops == 8
        and train_mask.shape[0] == 2
        and rngs % 2 == 0
        and steer_index.shape[1] <= 8
        and gate_dev % 8 == 0
        and gate_dev * rngs <= LANES
    )
    path = dual_shards if fits else plain_shards
    return path(raw_samples, filter_taps, range_code, train_mask, steer_index)


def solution(mesh):
    return jax.shard_map(
        shards,
        mesh=mesh,
        in_specs=(P("dop", "rng", None, None), P(), P(), P("dop", "rng"), P("dop", None)),
        out_specs=P(None, "dop", None, "rng"),
        check_vma=False,
    )
```
